256 devices in a mesh: seq: 64 (over z, x, core), head: 4 (over y).
Axes of the slice: x: 4, y: 4, z: 8, core: 2. Of those that a mesh axis runs over, the one named last changes fastest.
Arguments:
- frames: bfloat16 [131072, 1024], P('seq'), may hold values from -16 to 16
- text_states: bfloat16 [16384, 1024], P('seq'), may hold values from -48 to 48
- durations: int32 [64, 256], P('seq'), may hold values from 1 to 32, 2048 in all within a row
- w_query: bfloat16 [1024, 1024], P(None, 'head'), may hold values from -0.1875 to 0.1875
- w_key: bfloat16 [1024, 1024], P(None, 'head'), may hold values from -0.1875 to 0.1875
- w_value: bfloat16 [1024, 1024], P(None, 'head'), may hold values from -0.1875 to 0.1875
- w_out: bfloat16 [1024, 1024], P('head'), may hold values from -0.1875 to 0.1875
- cotangent: bfloat16 [131072, 1024], P('seq'), may hold values from -16 to 16
Outputs:
- layer_out: bfloat16 [131072, 1024], P(('seq', 'head'))
- frames_grad: bfloat16 [131072, 1024], P(('seq', 'head'))
- text_grad: bfloat16 [16384, 1024], P(('seq', 'head'))
- query_wgrad: float32 [1024, 1024], P('seq', 'head')
- key_wgrad: float32 [1024, 1024], P('seq', 'head')
- value_wgrad: float32 [1024, 1024], P('seq', 'head')
- out_wgrad: float32 [1024, 1024], P('head', 'seq')
The draws below stay inside these ranges and needn't reach their ends.
Inputs may be any that keep to these rules, and one draw needn't show every extreme that they name: `durations`: each row sums to 2048 and its largest entry is 32.
All inputs are finite; a program needn't handle non-finite values.
Results may differ from the reference program's by a relative error of at most 0.034.
The reference program's roundings to bfloat16 on the way count: a program that leaves them out, or rounds other values in their place, can miss the bound.
Values may be sent and summed in bfloat16 or wider, within the bound.
A program may use at most 128 MiB of HBM per device.

```python
import math
import jax
import jax.numpy as jnp
import numpy as np
from jax import lax

D = 1024
HEAD_DIM = 64
F_DEV = 2048
WINDOW = 32
DMAX = 32
S_DEV = 256
SHARDS = 64
FRAMES = 131072
TEXT = 16384
N_HEAD = 4


def draw_text_states(key, part):
    key = jax.random.fold_in(key, 5)
    first = jax.random.fold_in(key, 0)
    base = jax.random.truncated_normal(first, -4.0, 4.0, (TEXT, D), jnp.float32)
    return base.astype(jnp.bfloat16)


def with_spikes(entries, rng, source, target, parts, factor):
    owner, partner = [(jnp.arange(entries.shape[dim]) // (entries.shape[dim] // parts)).reshape([-1 if axis == dim else 1 for axis in range(entries.ndim)]) for dim in (source, target)]
    chosen = jax.random.permutation(rng, parts)[partner]
    strong = (owner == chosen) | (owner == (partner + parts // 2) % parts)
    return jnp.where(strong, factor * entries, entries)


def levels(stream_key, extent, cuts, smallest, high):
    level = 1.0
    for axis_at, parts in cuts:
        draws = jax.random.uniform(jax.random.fold_in(jax.random.fold_in(stream_key, 6), axis_at), (parts,), jnp.float32, smallest / len(cuts), high / len(cuts))
        level = level * jnp.repeat(jnp.exp(draws), extent[axis_at] // parts).reshape((-1,) + (1,) * (len(extent) - 1 - axis_at))
    return level


def profile(count, total, bound, skew):
    weights = [(1 << 20) // math.isqrt(rank ** skew) + 1 for rank in range(2, count + 1)]
    rest, given = total - bound - (count - 1), [1] * (count - 1)
    while rest > 0:
        candidates = [i for i in range(count - 1) if given[i] < bound]
        mass, left = sum([weights[i] for i in candidates]), rest
        for i in candidates:
            addition = min(bound - given[i], max(1, left * weights[i] // mass), rest)
            given[i] = given[i] + addition
            rest = rest - addition
    return np.array([bound] + given)


def ragged(own_key, count, total, limit, slope):
    if count == 2:
        one = jax.random.randint(own_key, (), max(1, total - limit), min(limit, total - 1) + 1)
        return jnp.stack([one, total - one])
    sizes = jnp.asarray(profile(count, total, limit, slope), jnp.int32)
    couples = (count - 1) // 2
    donor, receiver = sizes[1:1 + 2 * couples:2], sizes[2:2 + 2 * couples:2]
    room = jnp.minimum(donor - 1, limit - receiver)
    moved = jax.random.randint(jax.random.fold_in(own_key, 1), (couples,), 0, 1 << 20) % (room + 1)
    sizes = sizes.at[1:1 + 2 * couples:2].set(donor - moved).at[2:2 + 2 * couples:2].set(receiver + moved)
    return sizes[jax.random.permutation(jax.random.fold_in(own_key, 2), count)]


def noise(rng, shape, scale, reach, cuts=(), kind=jnp.bfloat16):
    result = jax.random.normal(rng, shape, jnp.float32) * scale
    if len(cuts) > 0:
        result = levels(rng, shape, cuts, -0.22, 0.18) * result
    return jnp.clip(result, min=-reach, max=reach).astype(kind)


def bell_draw_with(own_key, shape, scale, most, cuts, heavy, kind=jnp.bfloat16):
    array = scale * jax.random.normal(own_key, shape, jnp.float32)
    if cuts:
        array = array * levels(own_key, shape, cuts, -0.22, 0.18)
    return jnp.clip(with_spikes(array, jax.random.fold_in(own_key, 3), *heavy), -most, most).astype(kind)


def setup_inputs(seed: int = 0) -> dict:
    splits = jax.random.split(jax.random.key(seed), 9)
    frames = bell_draw_with(splits[0], (FRAMES, D), 1.0, 16.0, ((0, 64),), (0, 1, 64, 4.0))
    text_states = draw_text_states(jax.random.fold_in(splits[8], 71), 0)
    durations = jax.vmap(lambda own: ragged(own, S_DEV, F_DEV, DMAX, 2))(jax.random.split(splits[2], SHARDS)).reshape((SHARDS, S_DEV)).astype(jnp.int32)
    w_query = noise(splits[3], (D, D), D ** -0.5, 0.1875, ((1, 4),))
    w_key = noise(splits[4], (D, D), D ** -0.5, 0.1875, ((1, 4),))
    w_value = noise(splits[5], (D, D), D ** -0.5, 0.1875, ((1, 4),))
    w_out = noise(splits[6], (D, D), D ** -0.5, 0.1875, ((0, 4),))
    cotangent = bell_draw_with(splits[7], (FRAMES, D), 1.0, 16.0, ((0, 64),), (0, 1, 64, 4.0))
    return dict(frames=frames, text_states=text_states, durations=durations, w_query=w_query, w_key=w_key, w_value=w_value, w_out=w_out, cotangent=cotangent)


def band_mask(lengths_row, shard_index, frame_rows, text_rows, total_text):
    ends = jnp.cumsum(lengths_row, dtype=jnp.int32)
    positions = jnp.arange(frame_rows, dtype=jnp.int32)
    token_of = jnp.sum((ends[None, :] <= positions[:, None]).astype(jnp.int32), axis=1, dtype=jnp.int32)
    ext_index = jnp.arange(text_rows + 2 * WINDOW, dtype=jnp.int32)
    global_index = shard_index * text_rows - WINDOW + ext_index
    near = jnp.abs(ext_index[None, :] - WINDOW - token_of[:, None]) <= WINDOW
    inside = (global_index >= 0) & (global_index < total_text)
    return near & inside[None, :]


def attend_both(query, key_ext, val_ext, allowed, upstream):
    frame_rows = query.shape[0]
    ext_rows = key_ext.shape[0]
    head_count = query.shape[1] // HEAD_DIM
    attn_scale = HEAD_DIM ** -0.5
    query_heads = query.reshape(frame_rows, head_count, HEAD_DIM).astype(jnp.float32)
    key_heads = key_ext.reshape(ext_rows, head_count, HEAD_DIM).astype(jnp.float32)
    val_heads = val_ext.reshape(ext_rows, head_count, HEAD_DIM).astype(jnp.float32)
    scores = jnp.einsum('fhd,khd->hfk', query_heads, key_heads) * attn_scale
    scores = jnp.where(allowed[None], scores, -jnp.inf)
    largest = jnp.max(scores, axis=-1, keepdims=True)
    shifted = jnp.exp(scores - largest)
    prob = shifted / jnp.sum(shifted, axis=-1, keepdims=True)
    prob_b = prob.astype(jnp.bfloat16)
    attended = jnp.einsum('hfk,khd->fhd', prob_b.astype(jnp.float32), val_heads).astype(jnp.bfloat16)
    up_heads = upstream(attended.reshape(frame_rows, -1)).reshape(frame_rows, head_count, HEAD_DIM).astype(jnp.float32)
    dprob = jnp.einsum('fhd,khd->hfk', up_heads, val_heads)
    delta = jnp.sum(up_heads * attended.astype(jnp.float32), axis=2)
    dscore = (prob * (dprob - jnp.transpose(delta)[:, :, None]) * attn_scale).astype(jnp.bfloat16)
    dscore_f = dscore.astype(jnp.float32)
    dquery = jnp.einsum('hfk,khd->fhd', dscore_f, key_heads).astype(jnp.bfloat16).reshape(frame_rows, -1)
    dkey = jnp.einsum('hfk,fhd->khd', dscore_f, query_heads).reshape(ext_rows, -1)
    dval = jnp.einsum('hfk,fhd->khd', prob_b.astype(jnp.float32), up_heads).reshape(ext_rows, -1)
    return attended.reshape(frame_rows, -1), dquery, jnp.concatenate([dkey, dval], axis=1)


def grouped_sum(pairs):
    total = None
    for left, right in pairs:
        row_count = left.shape[0]
        out_cols = right.shape[0]
        width = left.shape[1] // N_HEAD
        term = jnp.einsum('rgk,ngk->grn', left.reshape(row_count, N_HEAD, width).astype(jnp.float32),
                          right.reshape(out_cols, N_HEAD, width).astype(jnp.float32))
        total = term if total is None else total + term
    rounded = lax.optimization_barrier(total.astype(jnp.bfloat16)).astype(jnp.float32)
    return jnp.sum(rounded, axis=0).astype(jnp.bfloat16)


def reference(frames, text_states, durations, w_query, w_key, w_value, w_out, cotangent):
    keys = jnp.dot(text_states, w_key, preferred_element_type=jnp.float32).astype(jnp.bfloat16)
    values = jnp.dot(text_states, w_value, preferred_element_type=jnp.float32).astype(jnp.bfloat16)
    zeros_rim = jnp.zeros((WINDOW, D), jnp.bfloat16)
    key_pad = jnp.concatenate([zeros_rim, keys, zeros_rim], axis=0)
    val_pad = jnp.concatenate([zeros_rim, values, zeros_rim], axis=0)
    out_t = jnp.transpose(w_out)

    def shard_work(shard_index):
        rows = lax.dynamic_slice_in_dim(frames, shard_index * F_DEV, F_DEV, 0)
        grad_rows = lax.dynamic_slice_in_dim(cotangent, shard_index * F_DEV, F_DEV, 0)
        query = jnp.dot(rows, w_query, preferred_element_type=jnp.float32).astype(jnp.bfloat16)
        key_ext = lax.dynamic_slice_in_dim(key_pad, shard_index * S_DEV, S_DEV + 2 * WINDOW, 0)
        val_ext = lax.dynamic_slice_in_dim(val_pad, shard_index * S_DEV, S_DEV + 2 * WINDOW, 0)
        lengths_row = lax.dynamic_index_in_dim(durations, shard_index, 0, keepdims=False)
        allowed = band_mask(lengths_row, shard_index, F_DEV, S_DEV, TEXT)

        def upstream(attended):
            return lax.dot_general(grad_rows, w_out, (((1,), (1,)), ((), ())),
                                   preferred_element_type=jnp.float32).astype(jnp.bfloat16)

        attended, dquery, grads_ext = attend_both(query, key_ext, val_ext, allowed, upstream)
        layer_rows = grouped_sum([(attended, out_t)])
        frame_grad_rows = grouped_sum([(dquery, w_query)])
        return attended, layer_rows, dquery, frame_grad_rows, grads_ext

    shard_ids = jnp.arange(SHARDS, dtype=jnp.int32)
    attended, layer_out, dquery, frames_grad, grads_ext = lax.map(shard_work, shard_ids)
    attended = attended.reshape(FRAMES, D)
    layer_out = layer_out.reshape(FRAMES, D)
    dquery = dquery.reshape(FRAMES, D)
    frames_grad = frames_grad.reshape(FRAMES, D)
    inner = grads_ext[:, WINDOW:WINDOW + S_DEV]
    lower = grads_ext[:, :WINDOW]
    upper = grads_ext[:, S_DEV + WINDOW:]
    empty = jnp.zeros((1, WINDOW, 2 * D), jnp.float32)
    from_above = jnp.concatenate([lower[1:], empty], axis=0)
    from_below = jnp.concatenate([empty, upper[:-1]], axis=0)
    inner = inner.at[:, :WINDOW].add(from_below)
    inner = inner.at[:, S_DEV - WINDOW:].add(from_above)
    kv_grad = inner.reshape(TEXT, 2 * D).astype(jnp.bfloat16)
    key_grad = kv_grad[:, :D]
    value_grad = kv_grad[:, D:]
    text_grad = grouped_sum([(key_grad, w_key), (value_grad, w_value)])
    dims = (((0,), (0,)), ((), ()))
    query_wgrad = lax.dot_general(frames, dquery, dims, preferred_element_type=jnp.float32)
    key_wgrad = lax.dot_general(text_states, key_grad, dims, preferred_element_type=jnp.float32)
    value_wgrad = lax.dot_general(text_states, value_grad, dims, preferred_element_type=jnp.float32)
    out_wgrad = lax.dot_general(attended, cotangent, dims, preferred_element_type=jnp.float32)
    return layer_out, frames_grad, text_grad, query_wgrad, key_wgrad, value_wgrad, out_wgrad
```

```python
import jax
import jax.numpy as jnp
from jax import lax
from jax.experimental import pallas as pl
from jax.experimental.pallas import tpu as pltpu
from jax.sharding import PartitionSpec as P

HEAD_DIM = 64
WINDOW = 32
HEADS = 4
COLS = HEADS * HEAD_DIM
D = 1024
F_DEV = 2048
S_DEV = 256
EXT = S_DEV + 2 * WINDOW
TILE = 512
SUB = 256
NARROW = 160
RANGES = 64
LOG2E = 1.4426950408889634
MESH = pl.DeviceIdType.MESH
BF = jnp.bfloat16
F32 = jnp.float32
NN = (((1,), (0,)), ((), ()))
NT = (((1,), (1,)), ((), ()))
TN = (((0,), (0,)), ((), ()))


def mm(left, right, dims):
    return lax.dot_general(left, right, dims, preferred_element_type=F32)


def attention_kernel(starts_ref, narrow_ref, frames_ref, cot_ref, text_ref, low_ref, high_ref,
                     wqt_ref, wk_ref, wv_ref, wo_ref, bounds_ref,
                     att_ref, dq_ref, gk_ref, gv_ref,
                     k_s, v_s, qt_s, ut_s):
    step = pl.program_id(0)

    @pl.when(step == 0)
    def _():
        text = jnp.concatenate([low_ref[...], text_ref[...], high_ref[...]], axis=0)
        keys = mm(text, wk_ref[...], NN).astype(BF)
        vals = mm(text, wv_ref[...], NN).astype(BF)
        for h in range(HEADS):
            k_s[h] = keys[:, h * HEAD_DIM:(h + 1) * HEAD_DIM]
            v_s[h] = vals[:, h * HEAD_DIM:(h + 1) * HEAD_DIM]
        gk_ref[...] = jnp.zeros_like(gk_ref)
        gv_ref[...] = jnp.zeros_like(gv_ref)

    qt_s[...] = mm(wqt_ref[...], frames_ref[...], NT).astype(BF)
    ut_s[...] = mm(wo_ref[...], cot_ref[...], NT).astype(BF)

    def process(sub, start, rows):
        lanes = pl.ds(sub * SUB, SUB)
        here = pl.ds(start, rows)
        low = bounds_ref[0:1, lanes]
        high = bounds_ref[1:2, lanes]
        state = lax.broadcasted_iota(jnp.int32, (rows, SUB), 0) + start
        allowed = (state >= low) & (state <= high)
        for h in range(HEADS):
            cols = pl.ds(h * HEAD_DIM, HEAD_DIM)
            q = qt_s[cols, lanes]
            u = ut_s[cols, lanes]
            k = k_s[h, here, :]
            v = v_s[h, here, :]
            s = jnp.where(allowed, mm(k, q, NN), -jnp.inf)
            top = jnp.max(s, axis=0, keepdims=True)
            e = jnp.exp2((s - top) * (LOG2E * HEAD_DIM ** -0.5))
            p = e * (1.0 / jnp.sum(e, axis=0, keepdims=True))
            pb = p.astype(BF)
            att = mm(v, pb, TN).astype(BF)
            att_ref[cols, lanes] = att
            delta = jnp.sum(u.astype(F32) * att.astype(F32), axis=0, keepdims=True)
            ds = (p * (mm(v, u, NN) - delta) * HEAD_DIM ** -0.5).astype(BF)
            dq_ref[cols, lanes] = mm(k, ds, TN).astype(BF)
            gk_ref[h, here, :] += mm(ds, q, NT)
            gv_ref[h, here, :] += mm(pb, u, NT)

    @pl.loop(0, TILE // SUB)
    def _(sub):
        index = step * (TILE // SUB) + sub
        start = pl.multiple_of(starts_ref[index], 16)

        @pl.when(narrow_ref[index] == 1)
        def _():
            process(sub, start, NARROW)

        @pl.when(narrow_ref[index] == 0)
        def _():
            process(sub, 0, EXT)


def attention(frames, cot, text, low, high, wqt, wk, wv, wo, bounds, starts, narrow):
    whole = lambda *shape: pl.BlockSpec(shape, lambda i, *_: (0,) * len(shape))
    return pl.pallas_call(
        attention_kernel,
        grid_spec=pltpu.PrefetchScalarGridSpec(
            num_scalar_prefetch=2,
            grid=(F_DEV // TILE,),
            in_specs=[
                pl.BlockSpec((TILE, D), lambda i, *_: (i, 0)),
                pl.BlockSpec((TILE, D), lambda i, *_: (i, 0)),
                whole(S_DEV, D), whole(WINDOW, D), whole(WINDOW, D),
                whole(COLS, D), whole(D, COLS), whole(D, COLS), whole(COLS, D),
                pl.BlockSpec((2, TILE), lambda i, *_: (0, i)),
            ],
            out_specs=[
                pl.BlockSpec((COLS, TILE), lambda i, *_: (0, i)),
                pl.BlockSpec((COLS, TILE), lambda i, *_: (0, i)),
                whole(HEADS, EXT, HEAD_DIM), whole(HEADS, EXT, HEAD_DIM),
            ],
            scratch_shapes=[
                pltpu.VMEM((HEADS, EXT, HEAD_DIM), BF),
                pltpu.VMEM((HEADS, EXT, HEAD_DIM), BF),
                pltpu.VMEM((COLS, TILE), BF),
                pltpu.VMEM((COLS, TILE), BF),
            ],
        ),
        out_shape=[
            jax.ShapeDtypeStruct((COLS, F_DEV), BF),
            jax.ShapeDtypeStruct((COLS, F_DEV), BF),
            jax.ShapeDtypeStruct((HEADS, EXT, HEAD_DIM), F32),
            jax.ShapeDtypeStruct((HEADS, EXT, HEAD_DIM), F32),
        ],
        compiler_params=pltpu.CompilerParams(vmem_limit_bytes=40 * 2 ** 20),
        cost_estimate=pl.CostEstimate(flops=8 * 10 ** 9, bytes_accessed=14 * 10 ** 6, transcendentals=3 * 10 ** 6),
    )(starts, narrow, frames, cot, text, low, high, wqt, wk, wv, wo, bounds)


def reduce_kernel(att_ref, dq_ref, inner_ref, edges_ref, text_ref, wk_ref, wv_ref, wall_ref, frames_hbm, cot_hbm,
                  layer_ref, fgrad_ref, tgrad_ref, wgrad_ref,
                  frames_s, cot_s, far_att, far_dq, far_edge, kv_s, term_s, near_s, sum_c, far_x, sum_x, far_z,
                  tterm_s, far_t, load_sem,
                  send_a, recv_a, send_e, recv_e, send_c, recv_c, send_x, recv_x, send_z, recv_z, send_t, recv_t):
    seq, head = lax.axis_index("seq"), lax.axis_index("head")
    core, x, z = seq % 2, (seq // 2) % 4, seq // 8
    rows_of = lambda d: (head + d) % 4
    x_of = lambda d: (x + d) % 4
    z_of = lambda d: (z + d) % 8
    at_y = lambda d: (seq, rows_of(d))
    at_x = lambda d: (z * 8 + x_of(d) * 2 + core, head)
    at_z = lambda d: (z_of(d) * 8 + x * 2 + core, head)
    at_core = (z * 8 + x * 2 + (1 - core), head)
    at_next = ((seq + 1) % RANGES, head)
    at_prev = ((seq + RANGES - 1) % RANGES, head)

    load_cot = pltpu.make_async_copy(cot_hbm, cot_s, load_sem.at[0])
    load_cot.start()
    load_frames = pltpu.make_async_copy(frames_hbm, frames_s, load_sem.at[1])
    load_frames.start()

    peers = [at_y(d) for d in (1, 2, 3)] + [at_x(d) for d in (1, 2, 3)] + [at_z(d) for d in range(1, 8)]
    peers += [at_core, at_next, at_prev]
    barrier = pltpu.get_barrier_semaphore()
    for peer in peers:
        pl.semaphore_signal(barrier, inc=1, device_id=peer, device_id_type=MESH)
    pl.semaphore_wait(barrier, len(peers))

    def send(src, dst, sends, recvs, index, peer):
        copy = pltpu.make_async_remote_copy(src_ref=src, dst_ref=dst, send_sem=sends.at[index], recv_sem=recvs.at[index],
                                            device_id=peer, device_id_type=MESH)
        copy.start()
        return copy

    edge_copies = [send(edges_ref.at[0], far_edge.at[0], send_e, recv_e, 0, at_prev),
                   send(edges_ref.at[1], far_edge.at[1], send_e, recv_e, 1, at_next)]
    att_copies, dq_copies = {}, {}
    for d in (2, 1, 3):
        lanes = pl.ds(pl.multiple_of(rows_of(d) * TILE, TILE), TILE)
        att_copies[d] = send(att_ref.at[:, lanes], far_att.at[d - 1], send_a, recv_a, d - 1, at_y(d))
    for d in (2, 1, 3):
        lanes = pl.ds(pl.multiple_of(rows_of(d) * TILE, TILE), TILE)
        dq_copies[d] = send(dq_ref.at[:, lanes], far_dq.at[d - 1], send_a, recv_a, d + 2, at_y(d))

    def put(group, width_at, value, block):
        for part in range(2):
            for chip in range(4):
                for side in range(2):
                    at = part * 128 + chip * 32 + side * 16
                    term_s[group, side, chip, block * 2 + part, :, :] = value[at:at + 16]

    def frame_term(group, left_ref, right_s):
        @pl.loop(0, 4)
        def _(block):
            lanes = pl.ds(pl.multiple_of(block * 256, 256), 256)
            value = mm(left_ref[...], right_s[:, lanes], NN)
            put(group, 0, jnp.transpose(value).astype(BF), block)

    def core_send(group):
        return send(term_s.at[group, 1 - core], near_s.at[group], send_c, recv_c, group, at_core)

    load_cot.wait()
    frame_term(0, att_ref, cot_s)
    core_copies = [core_send(0)]
    load_frames.wait()
    frame_term(1, dq_ref, frames_s)
    core_copies.append(core_send(1))
    for copy in edge_copies:
        copy.wait()
    kv_s[...] = inner_ref[...].astype(BF)
    kv_s[:WINDOW] = (inner_ref[:WINDOW] + far_edge[1].astype(F32)).astype(BF)
    kv_s[S_DEV - WINDOW:] = (inner_ref[S_DEV - WINDOW:] + far_edge[0].astype(F32)).astype(BF)

    for which in range(2):
        @pl.loop(0, 4)
        def _(block):
            lanes = pl.ds(pl.multiple_of(block * 256, 256), 256)
            value = mm(text_ref[:, lanes], kv_s[:, which * COLS:(which + 1) * COLS], TN)
            put(2 + which, 0, value.astype(BF), block)
        core_copies.append(core_send(2 + which))

    for part in range(4):
        rows = slice(part * 64, part * 64 + 64)
        value = mm(kv_s[rows, :COLS], wk_ref[...], NT) + mm(kv_s[rows, COLS:], wv_ref[...], NT)
        tterm_s[part] = value.astype(BF)
    text_copies = [send(tterm_s.at[rows_of(d)], far_t.at[d - 1], send_t, recv_t, d - 1, at_y(d)) for d in (2, 1, 3)]

    x_copies = []
    for group in range(4):
        core_copies[group].wait()

        @pl.loop(0, 4)
        def _(chip):
            sum_c[group, chip] = (term_s[group, core, chip].astype(F32) + near_s[group, chip].astype(F32)).astype(BF)
        x_copies.append([send(sum_c.at[group, x_of(d)], far_x.at[group, d - 1], send_x, recv_x, group * 3 + d - 1, at_x(d))
                         for d in (2, 1, 3)])

    z_copies = []
    for group in range(4):
        for copy in x_copies[group]:
            copy.wait()
        total = sum_c[group, x].astype(F32)
        for d in range(3):
            total = total + far_x[group, d].astype(F32)
        sum_x[group] = total.astype(BF)
        z_copies.append([send(sum_x.at[group, z_of(d)], far_z.at[group, d - 1], send_z, recv_z, group * 7 + d - 1, at_z(d))
                         for d in (4, 3, 5, 2, 6, 1, 7)])

    def project(mine_ref, far, first, out_ref):
        mine = pl.ds(pl.multiple_of(head * TILE, TILE), TILE)
        parts = [jnp.transpose(mine_ref[:, mine])] + [jnp.transpose(far[d - 1]) for d in (1, 2, 3)]
        origin = [head] + [(head + 4 - d) % 4 for d in (1, 2, 3)]
        for block in range(4):
            lanes = slice(block * 256, block * 256 + 256)
            total = None
            for part, source in zip(parts, origin):
                term = mm(part, wall_ref[source, first:first + COLS, lanes], NN).astype(BF).astype(F32)
                total = term if total is None else total + term
            out_ref[:, lanes] = total.astype(BF)

    for copy in att_copies.values():
        copy.wait()
    project(att_ref, far_att, 0, layer_ref)
    for copy in dq_copies.values():
        copy.wait()
    project(dq_ref, far_dq, COLS, fgrad_ref)

    for copy in text_copies:
        copy.wait()
    total = tterm_s[head].astype(F32)
    for d in range(3):
        total = total + far_t[d].astype(F32)
    tgrad_ref[...] = total.astype(BF)

    for group in range(4):
        for copy in z_copies[group]:
            copy.wait()
        total = sum_x[group, z].astype(F32)
        for d in range(7):
            total = total + far_z[group, d].astype(F32)
        wgrad_ref[group] = total


def reduce_all(att, dq, inner, edges, text, wk, wv, wall, frames, cot):
    vmem = pl.BlockSpec(memory_space=pltpu.VMEM)
    hbm = pl.BlockSpec(memory_space=pl.ANY)
    dma = pltpu.SemaphoreType.DMA
    return pl.pallas_call(
        reduce_kernel,
        in_specs=[vmem] * 8 + [hbm] * 2,
        out_specs=[vmem] * 4,
        out_shape=[
            jax.ShapeDtypeStruct((TILE, D), BF),
            jax.ShapeDtypeStruct((TILE, D), BF),
            jax.ShapeDtypeStruct((64, D), BF),
            jax.ShapeDtypeStruct((4, 16, COLS), F32),
        ],
        scratch_shapes=[
            pltpu.VMEM((F_DEV, D), BF),
            pltpu.VMEM((F_DEV, D), BF),
            pltpu.VMEM((3, COLS, TILE), BF),
            pltpu.VMEM((3, COLS, TILE), BF),
            pltpu.VMEM((2, WINDOW, 2 * COLS), BF),
            pltpu.VMEM((S_DEV, 2 * COLS), BF),
            pltpu.VMEM((4, 2, 4, 8, 16, COLS), BF),
            pltpu.VMEM((4, 4, 8, 16, COLS), BF),
            pltpu.VMEM((4, 4, 8, 16, COLS), BF),
            pltpu.VMEM((4, 3, 8, 16, COLS), BF),
            pltpu.VMEM((4, 8, 16, COLS), BF),
            pltpu.VMEM((4, 7, 16, COLS), BF),
            pltpu.VMEM((4, 64, D), BF),
            pltpu.VMEM((3, 64, D), BF),
            dma((2,)),
            dma((6,)), dma((6,)), dma((2,)), dma((2,)), dma((4,)), dma((4,)), dma((12,)), dma((12,)),
            dma((28,)), dma((28,)), dma((3,)), dma((3,)),
        ],
        compiler_params=pltpu.CompilerParams(collective_id=0, has_side_effects=True, vmem_limit_bytes=56 * 2 ** 20),
        cost_estimate=pl.CostEstimate(flops=7 * 10 ** 9, bytes_accessed=20 * 10 ** 6, transcendentals=0),
    )(att, dq, inner, edges, text, wk, wv, wall, frames, cot)


def on_device(frames, text_states, durations, w_query, w_key, w_value, w_out, cotangent):
    shard = lax.axis_index("seq")
    wqt = jnp.transpose(w_query)
    wall = lax.all_gather(jnp.concatenate([w_out, wqt], axis=0), "head", axis=0)
    low = lax.ppermute(text_states[S_DEV - WINDOW:], "seq", [(i, (i + 1) % RANGES) for i in range(RANGES)])
    high = lax.ppermute(text_states[:WINDOW], "seq", [(i, (i - 1) % RANGES) for i in range(RANGES)])

    ends = jnp.cumsum(durations[0], dtype=jnp.int32)
    own = jnp.sum((ends[:, None] <= jnp.arange(F_DEV, dtype=jnp.int32)[None, :]).astype(jnp.int32), axis=0, dtype=jnp.int32)
    first = jnp.where(shard == 0, WINDOW, 0)
    last = EXT - 1 - jnp.where(shard == RANGES - 1, WINDOW, 0)
    bounds = jnp.stack([jnp.maximum(own, first), jnp.minimum(own + 2 * WINDOW, last)])
    starts = jnp.minimum((own[::SUB] // 16) * 16, EXT - NARROW)
    narrow = (own[SUB - 1::SUB] + 2 * WINDOW < starts + NARROW).astype(jnp.int32)

    att, dq, gk, gv = attention(frames, cotangent, text_states, low, high, wqt, w_key, w_value, w_out, bounds, starts, narrow)
    both = jnp.concatenate([jnp.transpose(gk, (1, 0, 2)).reshape(EXT, COLS), jnp.transpose(gv, (1, 0, 2)).reshape(EXT, COLS)], axis=1)
    inner = both[WINDOW:WINDOW + S_DEV]
    edges = jnp.stack([both[:WINDOW], both[WINDOW + S_DEV:]]).astype(BF)
    layer, fgrad, tgrad, wgrad = reduce_all(att, dq, inner, edges, text_states, w_key, w_value, wall, frames, cotangent)
    return layer, fgrad, tgrad, wgrad[1], wgrad[2], wgrad[3], jnp.transpose(wgrad[0])


def solution(mesh):
    placed = (
        P("seq", None),
        P("seq", None),
        P("seq", None),
        P(None, "head"),
        P(None, "head"),
        P(None, "head"),
        P("head", None),
        P("seq", None),
    )
    return jax.shard_map(
        on_device,
        mesh=mesh,
        in_specs=placed,
        out_specs=(
            P(("seq", "head"), None),
            P(("seq", "head"), None),
            P(("seq", "head"), None),
            P("seq", "head"),
            P("seq", "head"),
            P("seq", "head"),
            P("head", "seq"),
        ),
        check_vma=False,
    )
```

```python
import jax
import jax.numpy as jnp
from jax import lax
from jax.experimental import pallas as pl
from jax.experimental.pallas import tpu as pltpu
from jax.sharding import PartitionSpec as P

HEAD_DIM = 64
WINDOW = 32
HEADS = 4
COLS = HEADS * HEAD_DIM
D = 1024
F_DEV = 2048
S_DEV = 256
EXT = S_DEV + 2 * WINDOW
TILE = 512
SUB = 256
SPAN = 272
RANGES = 64
LOG2E = 1.4426950408889634
MESH = pl.DeviceIdType.MESH
BF = jnp.bfloat16
F32 = jnp.float32
NN = (((1,), (0,)), ((), ()))
NT = (((1,), (1,)), ((), ()))
TN = (((0,), (0,)), ((), ()))


def mm(left, right, dims):
    return lax.dot_general(left, right, dims, preferred_element_type=F32)


def kernel(frames_hbm, cot_hbm, text_hbm, dur_ref, wq_hbm, wk_hbm, wv_hbm, wo_hbm,
           layer_ref, fgrad_ref, tgrad_ref, wgrad_ref,
           frames_s, cot_s, text_s, wq_s, wk_s, wv_s, wcat_s, wall_s,
           k_s, v_s, qt_s, ut_s, gk_s, gv_s, ends_s, att_s, dq_s,
           far_att, far_dq, edge_s, far_edge, kv_s, term_s, near_s, sum_c, far_x, sum_x, far_z, tterm_s, far_t,
           load_w, load_f, load_c,
           send_h, recv_h, send_wy, recv_wy, send_wx, recv_wx, send_wc, recv_wc,
           send_a, recv_a, send_b, recv_b, send_e, recv_e, send_c, recv_c, send_x, recv_x, send_z, recv_z, send_t, recv_t):
    seq, head = lax.axis_index("seq"), lax.axis_index("head")
    core, x, z = seq % 2, (seq // 2) % 4, seq // 8
    y_of = lambda d: (head + d) % 4
    x_of = lambda d: (x + d) % 4
    z_of = lambda d: (z + d) % 8
    at_y = lambda d: (seq, y_of(d))
    at_x = lambda d: (z * 8 + x_of(d) * 2 + core, head)
    at_z = lambda d: (z_of(d) * 8 + x * 2 + core, head)
    at_core = (z * 8 + x * 2 + (1 - core), head)
    at_next = ((seq + 1) % RANGES, head)
    at_prev = ((seq + RANGES - 1) % RANGES, head)

    peers = [at_y(d) for d in (1, 2, 3)] + [at_x(d) for d in (1, 2, 3)] + [at_z(d) for d in range(1, 8)]
    peers += [at_core, at_next, at_prev]
    barrier = pltpu.get_barrier_semaphore()
    for peer in peers:
        pl.semaphore_signal(barrier, inc=1, device_id=peer, device_id_type=MESH)

    def load(src, dst, sem):
        copy = pltpu.make_async_copy(src, dst, sem)
        copy.start()
        return copy

    loads = [load(wq_hbm, wq_s, load_w.at[0]),
             load(wo_hbm, wcat_s.at[0], load_w.at[1]),
             load(text_hbm, text_s.at[pl.ds(WINDOW, S_DEV)], load_w.at[2]),
             load(wk_hbm, wk_s, load_w.at[3]),
             load(wv_hbm, wv_s, load_w.at[4])]

    def chunk(j, which):
        rows = pl.ds(pl.multiple_of(((head + 1 + j) % 4) * TILE, TILE), TILE)
        if which == 0:
            return pltpu.make_async_copy(frames_hbm.at[rows], frames_s.at[rows], load_f.at[j])
        return pltpu.make_async_copy(cot_hbm.at[rows], cot_s.at[rows], load_c.at[j])

    for j in range(4):
        chunk(j, 0).start()
        chunk(j, 1).start()

    loads[0].wait()
    wcat_s[1] = jnp.transpose(wq_s[...])
    loads[1].wait()

    def remote(src, dst, sends, recvs, index, peer):
        return pltpu.make_async_remote_copy(src_ref=src, dst_ref=dst, send_sem=sends.at[index], recv_sem=recvs.at[index],
                                            device_id=peer, device_id_type=MESH)

    def send(*args):
        copy = remote(*args)
        copy.start()
        return copy

    pl.semaphore_wait(barrier, len(peers))
    halo = [send(text_hbm.at[pl.ds(S_DEV - WINDOW, WINDOW)], text_s.at[pl.ds(0, WINDOW)], send_h, recv_h, 0, at_next),
            send(text_hbm.at[pl.ds(0, WINDOW)], text_s.at[pl.ds(WINDOW + S_DEV, WINDOW)], send_h, recv_h, 1, at_prev)]
    quarter = pl.ds(pl.multiple_of(x * 64, 64), 64)
    from_y = [send(wcat_s.at[core, quarter], wall_s.at[head, core, quarter], send_wy, recv_wy, d - 1, at_y(d)) for d in (1, 2, 3)]

    length = dur_ref[...]
    before = lax.broadcasted_iota(jnp.int32, (S_DEV, S_DEV), 1) <= lax.broadcasted_iota(jnp.int32, (S_DEV, S_DEV), 0)
    ends_s[...] = jnp.sum(jnp.where(before, jnp.broadcast_to(length, (S_DEV, S_DEV)), 0), axis=1, keepdims=True)
    gk_s[...] = jnp.zeros_like(gk_s)
    gv_s[...] = jnp.zeros_like(gv_s)
    for copy in loads[2:]:
        copy.wait()
    for copy in halo:
        copy.wait()
    keys = mm(text_s[...], wk_s[...], NN).astype(BF)
    vals = mm(text_s[...], wv_s[...], NN).astype(BF)
    for h in range(HEADS):
        k_s[h] = keys[:, h * HEAD_DIM:(h + 1) * HEAD_DIM]
        v_s[h] = vals[:, h * HEAD_DIM:(h + 1) * HEAD_DIM]
    first = jnp.where(seq == 0, WINDOW, 0)
    last = EXT - 1 - jnp.where(seq == RANGES - 1, WINDOW, 0)

    def exchange(j, which):
        lanes = pl.ds(pl.multiple_of(((head + 1 + j) % 4) * TILE, TILE), TILE)
        peer = (seq, (head + 1 + j) % 4)
        if which == 0:
            return remote(att_s.at[:, lanes], far_att.at[j], send_a, recv_a, j, peer)
        return remote(dq_s.at[:, lanes], far_dq.at[j], send_b, recv_b, j, peer)

    from_x = []
    for d in (1, 2, 3):
        source = (head + 4 - d) % 4
        for e in (1, 2, 3):
            place = wall_s.at[source, core, quarter]
            from_x.append(remote(place, place, send_wx, recv_wx, (d - 1) * 3 + e - 1, at_x(e)))

    @pl.loop(0, 8)
    def _(i):
        j = i // 2
        tile = ((head + 1 + j) % 4) * 2 + i % 2

        @pl.when(i % 2 == 0)
        def _():
            chunk(j, 0).wait()
            chunk(j, 1).wait()

        rows = pl.ds(pl.multiple_of(tile * SUB, SUB), SUB)
        qt_s[...] = mm(wcat_s[1], frames_s[rows, :], NT).astype(BF)
        ut_s[...] = mm(wcat_s[0], cot_s[rows, :], NT).astype(BF)

        @pl.when(i == 0)
        def _():
            for d in range(3):
                from_y[d].wait()
            for copy in from_x:
                copy.start()

        start = pl.multiple_of((tile // 2) * 16, 16)
        here = pl.ds(start, SPAN)
        position = lax.broadcasted_iota(jnp.int32, (S_DEV, SUB), 1) + tile * SUB
        own = jnp.sum((ends_s[...] <= position).astype(jnp.int32), axis=0, keepdims=True)
        low = jnp.maximum(own, first)
        high = jnp.minimum(own + 2 * WINDOW, last)
        state = lax.broadcasted_iota(jnp.int32, (SPAN, SUB), 0) + start
        allowed = (state >= low) & (state <= high)
        hs = range(HEADS)
        cols = [pl.ds(h * HEAD_DIM, HEAD_DIM) for h in hs]
        q = [qt_s[cols[h], :] for h in hs]
        u = [ut_s[cols[h], :] for h in hs]
        k = [k_s[h, here, :] for h in hs]
        v = [v_s[h, here, :] for h in hs]
        s = [jnp.where(allowed, mm(k[h], q[h], NN), -jnp.inf) for h in hs]
        dp = [mm(v[h], u[h], NN) for h in hs]
        e = [jnp.exp2((s[h] - jnp.max(s[h], axis=0, keepdims=True)) * (LOG2E * HEAD_DIM ** -0.5)) for h in hs]
        p = [e[h] * (1.0 / jnp.sum(e[h], axis=0, keepdims=True)) for h in hs]
        pb = [p[h].astype(BF) for h in hs]
        att = [mm(v[h], pb[h], TN).astype(BF) for h in hs]
        for h in hs:
            att_s[cols[h], rows] = att[h]
        delta = [jnp.sum(u[h].astype(F32) * att[h].astype(F32), axis=0, keepdims=True) for h in hs]
        ds = [(p[h] * (dp[h] - delta[h]) * HEAD_DIM ** -0.5).astype(BF) for h in hs]
        for h in hs:
            gv_s[h, here, :] += mm(pb[h], u[h], NT)
        for h in hs:
            dq_s[cols[h], rows] = mm(k[h], ds[h], TN).astype(BF)
        for h in hs:
            gk_s[h, here, :] += mm(ds[h], q[h], NT)

        @pl.when((i % 2 == 1) & (i < 6))
        def _():
            exchange(j, 0).start()
            exchange(j, 1).start()

    for h in range(HEADS):
        cols = slice(h * HEAD_DIM, (h + 1) * HEAD_DIM)
        later = slice(COLS + h * HEAD_DIM, COLS + (h + 1) * HEAD_DIM)
        edge_s[0, :, cols] = gk_s[h, :WINDOW].astype(BF)
        edge_s[1, :, cols] = gk_s[h, WINDOW + S_DEV:].astype(BF)
        edge_s[0, :, later] = gv_s[h, :WINDOW].astype(BF)
        edge_s[1, :, later] = gv_s[h, WINDOW + S_DEV:].astype(BF)
    edge_copies = [send(edge_s.at[0], far_edge.at[0], send_e, recv_e, 0, at_prev),
                   send(edge_s.at[1], far_edge.at[1], send_e, recv_e, 1, at_next)]

    def put(group, value, block):
        for part in range(2):
            for chip in range(4):
                for side in range(2):
                    at = part * 128 + chip * 32 + side * 16
                    term_s[group, side, chip, block * 2 + part, :, :] = value[at:at + 16]

    def frame_term(group, left_s, right_s):
        @pl.loop(0, 4)
        def _(block):
            lanes = pl.ds(pl.multiple_of(block * 256, 256), 256)
            value = mm(left_s[...], right_s[:, lanes], NN)
            put(group, jnp.transpose(value).astype(BF), block)

    def core_send(group):
        return send(term_s.at[group, 1 - core], near_s.at[group], send_c, recv_c, group, at_core)

    frame_term(0, att_s, cot_s)
    core_copies = [core_send(0)]
    frame_term(1, dq_s, frames_s)
    core_copies.append(core_send(1))
    for copy in edge_copies:
        copy.wait()
    inner = slice(WINDOW, WINDOW + S_DEV)
    for h in range(HEADS):
        for at, grad in ((h * HEAD_DIM, gk_s), (COLS + h * HEAD_DIM, gv_s)):
            cols = slice(at, at + HEAD_DIM)
            grad[h, WINDOW:2 * WINDOW] += far_edge[1, :, cols].astype(F32)
            grad[h, S_DEV:WINDOW + S_DEV] += far_edge[0, :, cols].astype(F32)
            kv_s[:, cols] = grad[h, inner].astype(BF)

    for which in range(2):
        @pl.loop(0, 4)
        def _(block):
            lanes = pl.ds(pl.multiple_of(block * 256, 256), 256)
            value = mm(text_s[inner, lanes], kv_s[:, which * COLS:(which + 1) * COLS], TN)
            put(2 + which, value.astype(BF), block)
        core_copies.append(core_send(2 + which))

    for part in range(4):
        rows = slice(part * 64, part * 64 + 64)
        value = mm(kv_s[rows, :COLS], wk_s[...], NT) + mm(kv_s[rows, COLS:], wv_s[...], NT)
        tterm_s[part] = value.astype(BF)
    text_copies = [send(tterm_s.at[y_of(d)], far_t.at[d - 1], send_t, recv_t, d - 1, at_y(d)) for d in (2, 1, 3)]

    for copy in from_x:
        copy.wait()
    from_core = []
    for d in (1, 2, 3):
        place = wall_s.at[(head + 4 - d) % 4, core]
        from_core.append(send(place, place, send_wc, recv_wc, d - 1, at_core))

    x_copies = []
    for group in range(4):
        core_copies[group].wait()

        @pl.loop(0, 4)
        def _(chip):
            sum_c[group, chip] = (term_s[group, core, chip].astype(F32) + near_s[group, chip].astype(F32)).astype(BF)
        x_copies.append([send(sum_c.at[group, x_of(d)], far_x.at[group, d - 1], send_x, recv_x, group * 3 + d - 1, at_x(d))
                         for d in (2, 1, 3)])

    def project(mine_s, far, which, out_ref):
        mine = pl.ds(pl.multiple_of(head * TILE, TILE), TILE)
        parts = [jnp.transpose(mine_s[:, mine])] + [jnp.transpose(far[d - 1]) for d in (1, 2, 3)]
        for block in range(4):
            lanes = slice(block * 256, block * 256 + 256)
            total = mm(parts[0], wcat_s[which, :, lanes], NN).astype(BF).astype(F32)
            for d in (1, 2, 3):
                total = total + mm(parts[d], wall_s[(head + 4 - d) % 4, which, :, lanes], NN).astype(BF).astype(F32)
            out_ref[:, lanes] = total.astype(BF)

    for copy in from_core:
        copy.wait()
    for j in range(3):
        exchange(j, 0).wait()
    project(att_s, far_att, 0, layer_ref)
    for j in range(3):
        exchange(j, 1).wait()
    project(dq_s, far_dq, 1, fgrad_ref)

    z_copies = []
    for group in range(4):
        for copy in x_copies[group]:
            copy.wait()
        total = sum_c[group, x].astype(F32)
        for d in range(3):
            total = total + far_x[group, d].astype(F32)
        sum_x[group] = total.astype(BF)
        z_copies.append([send(sum_x.at[group, z_of(d)], far_z.at[group, d - 1], send_z, recv_z, group * 7 + d - 1, at_z(d))
                         for d in (4, 3, 5, 2, 6, 1, 7)])

    for copy in text_copies:
        copy.wait()
    total = tterm_s[head].astype(F32)
    for d in range(3):
        total = total + far_t[d].astype(F32)
    tgrad_ref[...] = total.astype(BF)

    for group in range(4):
        for copy in z_copies[group]:
            copy.wait()
        total = sum_x[group, z].astype(F32)
        for d in range(7):
            total = total + far_z[group, d].astype(F32)
        wgrad_ref[group] = total


def on_device(frames, text_states, durations, w_query, w_key, w_value, w_out, cotangent):
    vmem = pl.BlockSpec(memory_space=pltpu.VMEM)
    hbm = pl.BlockSpec(memory_space=pl.ANY)
    dma = pltpu.SemaphoreType.DMA
    layer, fgrad, tgrad, wgrad = pl.pallas_call(
        kernel,
        in_specs=[hbm] * 3 + [vmem] + [hbm] * 4,
        out_specs=[vmem] * 4,
        out_shape=[
            jax.ShapeDtypeStruct((TILE, D), BF),
            jax.ShapeDtypeStruct((TILE, D), BF),
            jax.ShapeDtypeStruct((64, D), BF),
            jax.ShapeDtypeStruct((4, 16, COLS), F32),
        ],
        scratch_shapes=[
            pltpu.VMEM((F_DEV, D), BF),
            pltpu.VMEM((F_DEV, D), BF),
            pltpu.VMEM((EXT, D), BF),
            pltpu.VMEM((D, COLS), BF),
            pltpu.VMEM((D, COLS), BF),
            pltpu.VMEM((D, COLS), BF),
            pltpu.VMEM((2, COLS, D), BF),
            pltpu.VMEM((4, 2, COLS, D), BF),
            pltpu.VMEM((HEADS, EXT, HEAD_DIM), BF),
            pltpu.VMEM((HEADS, EXT, HEAD_DIM), BF),
            pltpu.VMEM((COLS, SUB), BF),
            pltpu.VMEM((COLS, SUB), BF),
            pltpu.VMEM((HEADS, EXT, HEAD_DIM), F32),
            pltpu.VMEM((HEADS, EXT, HEAD_DIM), F32),
            pltpu.VMEM((S_DEV, 1), jnp.int32),
            pltpu.VMEM((COLS, F_DEV), BF),
            pltpu.VMEM((COLS, F_DEV), BF),
            pltpu.VMEM((3, COLS, TILE), BF),
            pltpu.VMEM((3, COLS, TILE), BF),
            pltpu.VMEM((2, WINDOW, 2 * COLS), BF),
            pltpu.VMEM((2, WINDOW, 2 * COLS), BF),
            pltpu.VMEM((S_DEV, 2 * COLS), BF),
            pltpu.VMEM((4, 2, 4, 8, 16, COLS), BF),
            pltpu.VMEM((4, 4, 8, 16, COLS), BF),
            pltpu.VMEM((4, 4, 8, 16, COLS), BF),
            pltpu.VMEM((4, 3, 8, 16, COLS), BF),
            pltpu.VMEM((4, 8, 16, COLS), BF),
            pltpu.VMEM((4, 7, 16, COLS), BF),
            pltpu.VMEM((4, 64, D), BF),
            pltpu.VMEM((3, 64, D), BF),
            dma((5,)), dma((4,)), dma((4,)),
            dma((2,)), dma((2,)), dma((3,)), dma((3,)), dma((9,)), dma((9,)), dma((3,)), dma((3,)),
            dma((3,)), dma((3,)), dma((3,)), dma((3,)), dma((2,)), dma((2,)), dma((4,)), dma((4,)),
            dma((12,)), dma((12,)), dma((28,)), dma((28,)), dma((3,)), dma((3,)),
        ],
        compiler_params=pltpu.CompilerParams(collective_id=0, has_side_effects=True, vmem_limit_bytes=60 * 2 ** 20),
        cost_estimate=pl.CostEstimate(flops=15 * 10 ** 9, bytes_accessed=16 * 10 ** 6, transcendentals=3 * 10 ** 6),
    )(frames, cotangent, text_states, durations, w_query, w_key, w_value, w_out)
    return layer, fgrad, tgrad, wgrad[1], wgrad[2], wgrad[3], jnp.transpose(wgrad[0])


def solution(mesh):
    placed = (
        P("seq", None),
        P("seq", None),
        P("seq", None),
        P(None, "head"),
        P(None, "head"),
        P(None, "head"),
        P("head", None),
        P("seq", None),
    )
    return jax.shard_map(
        on_device,
        mesh=mesh,
        in_specs=placed,
        out_specs=(
            P(("seq", "head"), None),
            P(("seq", "head"), None),
            P(("seq", "head"), None),
            P("seq", "head"),
            P("seq", "head"),
            P("seq", "head"),
            P("head", "seq"),
        ),
        check_vma=False,
    )
```

```python
import jax
import jax.numpy as jnp
from jax import lax
from jax.experimental import pallas as pl
from jax.experimental.pallas import tpu as pltpu
from jax.sharding import PartitionSpec as P

HEAD_DIM = 64
WINDOW = 32
HEADS = 4
COLS = HEADS * HEAD_DIM
D = 1024
F_DEV = 2048
S_DEV = 256
EXT = S_DEV + 2 * WINDOW
TILE = 512
SUB = 256
SPAN = 272
RANGES = 64
LOG2E = 1.4426950408889634
MESH = pl.DeviceIdType.MESH
BF = jnp.bfloat16
F32 = jnp.float32
NN = (((1,), (0,)), ((), ()))
NT = (((1,), (1,)), ((), ()))
TN = (((0,), (0,)), ((), ()))


def mm(left, right, dims):
    return lax.dot_general(left, right, dims, preferred_element_type=F32)


def kernel(frames_hbm, cot_hbm, text_hbm, dur_ref, wq_hbm, wk_hbm, wv_hbm, wo_hbm,
           layer_hbm, fgrad_hbm, tgrad_hbm, wgrad_hbm,
           layer_s, fgrad_s, tgrad_s, wgrad_s,
           frames_s, cot_s, text_s, wq_s, wk_s, wv_s, wcat_s, wall_s,
           k_s, v_s, qt_s, ut_s, gk_s, gv_s, ends_s, att_s, dq_s,
           far_att, far_dq, edge_s, far_edge, kv_s, term_s, near_s, sum_c, far_x, sum_x, far_z, tterm_s, far_t,
           load_w, load_f, load_c, store_sem,
           send_h, recv_h, send_wy, recv_wy, send_wx, recv_wx, send_wc, recv_wc,
           send_a, recv_a, send_b, recv_b, send_e, recv_e, send_c, recv_c, send_x, recv_x, send_z, recv_z, send_t, recv_t):
    seq, head = lax.axis_index("seq"), lax.axis_index("head")
    core, x, z = seq % 2, (seq // 2) % 4, seq // 8
    y_of = lambda d: (head + d) % 4
    x_of = lambda d: (x + d) % 4
    z_of = lambda d: (z + d) % 8
    at_y = lambda d: (seq, y_of(d))
    at_x = lambda d: (z * 8 + x_of(d) * 2 + core, head)
    at_z = lambda d: (z_of(d) * 8 + x * 2 + core, head)
    at_core = (z * 8 + x * 2 + (1 - core), head)
    at_next = ((seq + 1) % RANGES, head)
    at_prev = ((seq + RANGES - 1) % RANGES, head)

    peers = [at_y(d) for d in (1, 2, 3)] + [at_x(d) for d in (1, 2, 3)] + [at_z(d) for d in range(1, 8)]
    peers += [at_core, at_next, at_prev]
    barrier = pltpu.get_barrier_semaphore()
    for peer in peers:
        pl.semaphore_signal(barrier, inc=1, device_id=peer, device_id_type=MESH)

    def load(src, dst, sem):
        copy = pltpu.make_async_copy(src, dst, sem)
        copy.start()
        return copy

    loads = [load(wq_hbm, wq_s, load_w.at[0]),
             load(wo_hbm, wcat_s.at[0], load_w.at[1]),
             load(text_hbm, text_s.at[pl.ds(WINDOW, S_DEV)], load_w.at[2]),
             load(wk_hbm, wk_s, load_w.at[3]),
             load(wv_hbm, wv_s, load_w.at[4])]

    def chunk(j, which):
        rows = pl.ds(pl.multiple_of(((head + 1 + j) % 4) * TILE, TILE), TILE)
        if which == 0:
            return pltpu.make_async_copy(frames_hbm.at[rows], frames_s.at[rows], load_f.at[j])
        return pltpu.make_async_copy(cot_hbm.at[rows], cot_s.at[rows], load_c.at[j])

    for j in range(4):
        chunk(j, 0).start()
        chunk(j, 1).start()

    loads[0].wait()
    wcat_s[1] = jnp.transpose(wq_s[...])
    loads[1].wait()

    def remote(src, dst, sends, recvs, index, peer):
        return pltpu.make_async_remote_copy(src_ref=src, dst_ref=dst, send_sem=sends.at[index], recv_sem=recvs.at[index],
                                            device_id=peer, device_id_type=MESH)

    def send(*args):
        copy = remote(*args)
        copy.start()
        return copy

    pl.semaphore_wait(barrier, len(peers))
    halo = [send(text_hbm.at[pl.ds(S_DEV - WINDOW, WINDOW)], text_s.at[pl.ds(0, WINDOW)], send_h, recv_h, 0, at_next),
            send(text_hbm.at[pl.ds(0, WINDOW)], text_s.at[pl.ds(WINDOW + S_DEV, WINDOW)], send_h, recv_h, 1, at_prev)]
    quarter = pl.ds(pl.multiple_of(x * 64, 64), 64)
    from_y = [send(wcat_s.at[core, quarter], wall_s.at[head, core, quarter], send_wy, recv_wy, d - 1, at_y(d)) for d in (1, 2, 3)]

    @pl.loop(0, 4)
    def _(j):
        chunk(j, 0).wait()
        chunk(j, 1).wait()
        rows = pl.ds(pl.multiple_of(((head + 1 + j) % 4) * TILE, TILE), TILE)
        qt_s[:, rows] = mm(wcat_s[1], frames_s[rows, :], NT).astype(BF)
        ut_s[:, rows] = mm(wcat_s[0], cot_s[rows, :], NT).astype(BF)

    length = dur_ref[...]
    before = lax.broadcasted_iota(jnp.int32, (S_DEV, S_DEV), 1) <= lax.broadcasted_iota(jnp.int32, (S_DEV, S_DEV), 0)
    ends_s[...] = jnp.sum(jnp.where(before, jnp.broadcast_to(length, (S_DEV, S_DEV)), 0), axis=1, keepdims=True)
    gk_s[...] = jnp.zeros_like(gk_s)
    gv_s[...] = jnp.zeros_like(gv_s)
    for copy in loads[2:]:
        copy.wait()
    for copy in halo:
        copy.wait()
    keys = mm(text_s[...], wk_s[...], NN).astype(BF)
    vals = mm(text_s[...], wv_s[...], NN).astype(BF)
    for h in range(HEADS):
        k_s[h] = keys[:, h * HEAD_DIM:(h + 1) * HEAD_DIM]
        v_s[h] = vals[:, h * HEAD_DIM:(h + 1) * HEAD_DIM]
    first = jnp.where(seq == 0, WINDOW, 0)
    last = EXT - 1 - jnp.where(seq == RANGES - 1, WINDOW, 0)

    def exchange(i, which):
        lanes = pl.ds(pl.multiple_of(((head + 1 + i // 2) % 4) * TILE + (i % 2) * SUB, SUB), SUB)
        there = pl.ds(pl.multiple_of((i % 2) * SUB, SUB), SUB)
        peer = (seq, (head + 1 + i // 2) % 4)
        if which == 0:
            return remote(att_s.at[:, lanes], far_att.at[i // 2, :, there], send_a, recv_a, i, peer)
        return remote(dq_s.at[:, lanes], far_dq.at[i // 2, :, there], send_b, recv_b, i, peer)

    from_x = []
    for d in (1, 2, 3):
        source = (head + 4 - d) % 4
        from_y[d - 1].wait()
        for e in (1, 2, 3):
            place = wall_s.at[source, core, quarter]
            from_x.append(send(place, place, send_wx, recv_wx, (d - 1) * 3 + e - 1, at_x(e)))

    @pl.loop(0, 8)
    def _(i):
        tile = ((head + 1 + i // 2) % 4) * 2 + i % 2

        rows = pl.ds(pl.multiple_of(tile * SUB, SUB), SUB)
        start = pl.multiple_of((tile // 2) * 16, 16)
        here = pl.ds(start, SPAN)
        position = lax.broadcasted_iota(jnp.int32, (S_DEV, SUB), 1) + tile * SUB
        own = jnp.sum((ends_s[...] <= position).astype(jnp.int32), axis=0, keepdims=True)
        low = jnp.maximum(own, first)
        high = jnp.minimum(own + 2 * WINDOW, last)
        state = lax.broadcasted_iota(jnp.int32, (SPAN, SUB), 0) + start
        allowed = (state >= low) & (state <= high)
        hs = range(HEADS)
        cols = [pl.ds(h * HEAD_DIM, HEAD_DIM) for h in hs]
        q = [qt_s[cols[h], rows] for h in hs]
        u = [ut_s[cols[h], rows] for h in hs]
        k = [k_s[h, here, :] for h in hs]
        v = [v_s[h, here, :] for h in hs]
        s = [jnp.where(allowed, mm(k[h], q[h], NN), -jnp.inf) for h in hs]
        dp = [mm(v[h], u[h], NN) for h in hs]
        e = [jnp.exp2((s[h] - jnp.max(s[h], axis=0, keepdims=True)) * (LOG2E * HEAD_DIM ** -0.5)) for h in hs]
        p = [e[h] * (1.0 / jnp.sum(e[h], axis=0, keepdims=True)) for h in hs]
        pb = [p[h].astype(BF) for h in hs]
        att = [mm(v[h], pb[h], TN).astype(BF) for h in hs]
        for h in hs:
            att_s[cols[h], rows] = att[h]
        delta = [jnp.sum(u[h].astype(F32) * att[h].astype(F32), axis=0, keepdims=True) for h in hs]
        ds = [(p[h] * (dp[h] - delta[h]) * HEAD_DIM ** -0.5).astype(BF) for h in hs]
        for h in hs:
            gv_s[h, here, :] += mm(pb[h], u[h], NT)
        for h in hs:
            dq_s[cols[h], rows] = mm(k[h], ds[h], TN).astype(BF)
        for h in hs:
            gk_s[h, here, :] += mm(ds[h], q[h], NT)

        @pl.when(i < 6)
        def _():
            exchange(i, 0).start()
            exchange(i, 1).start()

    for h in range(HEADS):
        cols = slice(h * HEAD_DIM, (h + 1) * HEAD_DIM)
        later = slice(COLS + h * HEAD_DIM, COLS + (h + 1) * HEAD_DIM)
        edge_s[0, :, cols] = gk_s[h, :WINDOW].astype(BF)
        edge_s[1, :, cols] = gk_s[h, WINDOW + S_DEV:].astype(BF)
        edge_s[0, :, later] = gv_s[h, :WINDOW].astype(BF)
        edge_s[1, :, later] = gv_s[h, WINDOW + S_DEV:].astype(BF)
    edge_copies = [send(edge_s.at[0], far_edge.at[0], send_e, recv_e, 0, at_prev),
                   send(edge_s.at[1], far_edge.at[1], send_e, recv_e, 1, at_next)]

    def put(group, value, block):
        for part in range(2):
            for chip in range(4):
                for side in range(2):
                    at = part * 128 + chip * 32 + side * 16
                    term_s[group, side, chip, block * 2 + part, :, :] = value[at:at + 16]

    def frame_term(group, left_s, right_s):
        @pl.loop(0, 4)
        def _(block):
            lanes = pl.ds(pl.multiple_of(block * 256, 256), 256)
            value = mm(left_s[...], right_s[:, lanes], NN)
            put(group, jnp.transpose(value).astype(BF), block)

    def core_send(group):
        return send(term_s.at[group, 1 - core], near_s.at[group], send_c, recv_c, group, at_core)

    x_copies = []

    def chip_sum(group):
        core_copies[group].wait()

        @pl.loop(0, 4)
        def _(chip):
            sum_c[group, chip] = (term_s[group, core, chip].astype(F32) + near_s[group, chip].astype(F32)).astype(BF)
        x_copies.append([send(sum_c.at[group, x_of(d)], far_x.at[group, d - 1], send_x, recv_x, group * 3 + d - 1, at_x(d))
                         for d in (2, 1, 3)])

    frame_term(0, att_s, cot_s)
    core_copies = [core_send(0)]
    frame_term(1, dq_s, frames_s)
    core_copies.append(core_send(1))
    for copy in edge_copies:
        copy.wait()
    inner = slice(WINDOW, WINDOW + S_DEV)
    for h in range(HEADS):
        for at, grad in ((h * HEAD_DIM, gk_s), (COLS + h * HEAD_DIM, gv_s)):
            cols = slice(at, at + HEAD_DIM)
            grad[h, WINDOW:2 * WINDOW] += far_edge[1, :, cols].astype(F32)
            grad[h, S_DEV:WINDOW + S_DEV] += far_edge[0, :, cols].astype(F32)
            kv_s[:, cols] = grad[h, inner].astype(BF)
    chip_sum(0)

    for which in range(2):
        @pl.loop(0, 4)
        def _(block):
            lanes = pl.ds(pl.multiple_of(block * 256, 256), 256)
            value = mm(text_s[inner, lanes], kv_s[:, which * COLS:(which + 1) * COLS], TN)
            put(2 + which, value.astype(BF), block)
        core_copies.append(core_send(2 + which))
    chip_sum(1)

    for part in range(4):
        rows = slice(part * 64, part * 64 + 64)
        value = mm(kv_s[rows, :COLS], wk_s[...], NT) + mm(kv_s[rows, COLS:], wv_s[...], NT)
        tterm_s[part] = value.astype(BF)
    text_copies = [send(tterm_s.at[y_of(d)], far_t.at[d - 1], send_t, recv_t, d - 1, at_y(d)) for d in (2, 1, 3)]
    chip_sum(2)
    chip_sum(3)

    for copy in from_x:
        copy.wait()
    from_core = []
    for d in (1, 2, 3):
        place = wall_s.at[(head + 4 - d) % 4, core]
        from_core.append(send(place, place, send_wc, recv_wc, d - 1, at_core))

    z_copies = []
    for group in range(4):
        for copy in x_copies[group]:
            copy.wait()
        total = sum_c[group, x].astype(F32)
        for d in range(3):
            total = total + far_x[group, d].astype(F32)
        sum_x[group] = total.astype(BF)
        z_copies.append([send(sum_x.at[group, z_of(d)], far_z.at[group, d - 1], send_z, recv_z, group * 7 + d - 1, at_z(d))
                         for d in (4, 3, 5, 2, 6, 1, 7)])

    def project(mine_s, far, which, out_s):
        mine = pl.ds(pl.multiple_of(head * TILE, TILE), TILE)
        parts = [jnp.transpose(mine_s[:, mine])] + [jnp.transpose(far[d - 1]) for d in (1, 2, 3)]
        for block in range(4):
            lanes = slice(block * 256, block * 256 + 256)
            total = mm(parts[0], wcat_s[which, :, lanes], NN).astype(BF).astype(F32)
            for d in (1, 2, 3):
                total = total + mm(parts[d], wall_s[(head + 4 - d) % 4, which, :, lanes], NN).astype(BF).astype(F32)
            out_s[:, lanes] = total.astype(BF)

    for copy in from_core:
        copy.wait()
    for i in range(6):
        exchange(i, 0).wait()
    project(att_s, far_att, 0, layer_s)
    stores = [load(layer_s, layer_hbm, store_sem.at[0])]
    for i in range(6):
        exchange(i, 1).wait()
    project(dq_s, far_dq, 1, fgrad_s)
    stores.append(load(fgrad_s, fgrad_hbm, store_sem.at[1]))

    for copy in text_copies:
        copy.wait()
    total = tterm_s[head].astype(F32)
    for d in range(3):
        total = total + far_t[d].astype(F32)
    tgrad_s[...] = total.astype(BF)
    stores.append(load(tgrad_s, tgrad_hbm, store_sem.at[2]))

    for group in range(4):
        for copy in z_copies[group]:
            copy.wait()
        total = sum_x[group, z].astype(F32)
        for d in range(7):
            total = total + far_z[group, d].astype(F32)
        wgrad_s[group] = total
    stores.append(load(wgrad_s, wgrad_hbm, store_sem.at[3]))
    for copy in stores:
        copy.wait()


def move_kernel(layer_in, fgrad_in, tgrad_in, wgrad_in, layer_out, fgrad_out, tgrad_out, w0, w1, w2, w3,
                layer_s, fgrad_s, tgrad_s, wgrad_s, into, out_of):
    pieces = []
    for part in range(4):
        rows = pl.ds(part * 128, 128)
        pieces.append((layer_in.at[rows], layer_s.at[rows], layer_out.at[rows]))
        pieces.append((fgrad_in.at[rows], fgrad_s.at[rows], fgrad_out.at[rows]))
    pieces.append((tgrad_in, tgrad_s, tgrad_out))
    for group, out in enumerate((w0, w1, w2, w3)):
        pieces.append((wgrad_in.at[group], wgrad_s.at[group], out))
    reads = [pltpu.make_async_copy(src, mid, into.at[n]) for n, (src, mid, _) in enumerate(pieces)]
    writes = [pltpu.make_async_copy(mid, dst, out_of.at[n]) for n, (_, mid, dst) in enumerate(pieces)]
    for copy in reads:
        copy.start()
    for read, write in zip(reads, writes):
        read.wait()
        write.start()
    for copy in writes:
        copy.wait()


def on_device(frames, text_states, durations, w_query, w_key, w_value, w_out, cotangent):
    vmem = pl.BlockSpec(memory_space=pltpu.VMEM)
    hbm = pl.BlockSpec(memory_space=pltpu.HBM)
    dma = pltpu.SemaphoreType.DMA
    layer, fgrad, tgrad, wgrad = pl.pallas_call(
        kernel,
        in_specs=[hbm] * 3 + [vmem] + [hbm] * 4,
        out_specs=[hbm] * 4,
        out_shape=[
            jax.ShapeDtypeStruct((TILE, D), BF),
            jax.ShapeDtypeStruct((TILE, D), BF),
            jax.ShapeDtypeStruct((64, D), BF),
            jax.ShapeDtypeStruct((4, 16, COLS), F32),
        ],
        scratch_shapes=[
            pltpu.VMEM((TILE, D), BF),
            pltpu.VMEM((TILE, D), BF),
            pltpu.VMEM((64, D), BF),
            pltpu.VMEM((4, 16, COLS), F32),
            pltpu.VMEM((F_DEV, D), BF),
            pltpu.VMEM((F_DEV, D), BF),
            pltpu.VMEM((EXT, D), BF),
            pltpu.VMEM((D, COLS), BF),
            pltpu.VMEM((D, COLS), BF),
            pltpu.VMEM((D, COLS), BF),
            pltpu.VMEM((2, COLS, D), BF),
            pltpu.VMEM((4, 2, COLS, D), BF),
            pltpu.VMEM((HEADS, EXT, HEAD_DIM), BF),
            pltpu.VMEM((HEADS, EXT, HEAD_DIM), BF),
            pltpu.VMEM((COLS, F_DEV), BF),
            pltpu.VMEM((COLS, F_DEV), BF),
            pltpu.VMEM((HEADS, EXT, HEAD_DIM), F32),
            pltpu.VMEM((HEADS, EXT, HEAD_DIM), F32),
            pltpu.VMEM((S_DEV, 1), jnp.int32),
            pltpu.VMEM((COLS, F_DEV), BF),
            pltpu.VMEM((COLS, F_DEV), BF),
            pltpu.VMEM((3, COLS, TILE), BF),
            pltpu.VMEM((3, COLS, TILE), BF),
            pltpu.VMEM((2, WINDOW, 2 * COLS), BF),
            pltpu.VMEM((2, WINDOW, 2 * COLS), BF),
            pltpu.VMEM((S_DEV, 2 * COLS), BF),
            pltpu.VMEM((4, 2, 4, 8, 16, COLS), BF),
            pltpu.VMEM((4, 4, 8, 16, COLS), BF),
            pltpu.VMEM((4, 4, 8, 16, COLS), BF),
            pltpu.VMEM((4, 3, 8, 16, COLS), BF),
            pltpu.VMEM((4, 8, 16, COLS), BF),
            pltpu.VMEM((4, 7, 16, COLS), BF),
            pltpu.VMEM((4, 64, D), BF),
            pltpu.VMEM((3, 64, D), BF),
            dma((5,)), dma((4,)), dma((4,)), dma((4,)),
            dma((2,)), dma((2,)), dma((3,)), dma((3,)), dma((9,)), dma((9,)), dma((3,)), dma((3,)),
            dma((6,)), dma((6,)), dma((6,)), dma((6,)), dma((2,)), dma((2,)), dma((4,)), dma((4,)),
            dma((12,)), dma((12,)), dma((28,)), dma((28,)), dma((3,)), dma((3,)),
        ],
        compiler_params=pltpu.CompilerParams(collective_id=0, has_side_effects=True, vmem_limit_bytes=60 * 2 ** 20),
        cost_estimate=pl.CostEstimate(flops=15 * 10 ** 9, bytes_accessed=16 * 10 ** 6, transcendentals=3 * 10 ** 6),
    )(frames, cotangent, text_states, durations, w_query, w_key, w_value, w_out)
    small = jax.ShapeDtypeStruct((16, COLS), F32)
    layer, fgrad, tgrad, w0, w1, w2, w3 = pl.pallas_call(
        move_kernel,
        in_specs=[hbm] * 4,
        out_specs=[hbm] * 7,
        out_shape=[
            jax.ShapeDtypeStruct((TILE, D), BF),
            jax.ShapeDtypeStruct((TILE, D), BF),
            jax.ShapeDtypeStruct((64, D), BF),
            small, small, small, small,
        ],
        scratch_shapes=[
            pltpu.VMEM((TILE, D), BF),
            pltpu.VMEM((TILE, D), BF),
            pltpu.VMEM((64, D), BF),
            pltpu.VMEM((4, 16, COLS), F32),
            dma((13,)), dma((13,)),
        ],
        compiler_params=pltpu.CompilerParams(vmem_limit_bytes=60 * 2 ** 20),
        cost_estimate=pl.CostEstimate(flops=0, bytes_accessed=5 * 10 ** 6, transcendentals=0),
    )(layer, fgrad, tgrad, wgrad)
    return layer, fgrad, tgrad, w1, w2, w3, jnp.transpose(w0)


def solution(mesh):
    placed = (
        P("seq", None),
        P("seq", None),
        P("seq", None),
        P(None, "head"),
        P(None, "head"),
        P(None, "head"),
        P("head", None),
        P("seq", None),
    )
    return jax.shard_map(
        on_device,
        mesh=mesh,
        in_specs=placed,
        out_specs=(
            P(("seq", "head"), None),
            P(("seq", "head"), None),
            P(("seq", "head"), None),
            P("seq", "head"),
            P("seq", "head"),
            P("seq", "head"),
            P("head", "seq"),
        ),
        check_vma=False,
    )
```

```python
import jax
import jax.numpy as jnp
from jax import lax
from jax.experimental import pallas as pl
from jax.experimental.pallas import tpu as pltpu
from jax.sharding import PartitionSpec as P

HEAD_DIM = 64
WINDOW = 32
HEADS = 4
COLS = HEADS * HEAD_DIM
D = 1024
F_DEV = 2048
S_DEV = 256
EXT = S_DEV + 2 * WINDOW
TILE = 512
SUB = 256
SPAN = 272
RANGES = 64
LOG2E = 1.4426950408889634
MESH = pl.DeviceIdType.MESH
BF = jnp.bfloat16
F32 = jnp.float32
NN = (((1,), (0,)), ((), ()))
NT = (((1,), (1,)), ((), ()))
TN = (((0,), (0,)), ((), ()))


def mm(left, right, dims):
    return lax.dot_general(left, right, dims, preferred_element_type=F32)


def kernel(frames_hbm, cot_hbm, text_hbm, dur_ref, wq_hbm, wk_hbm, wv_hbm, wo_hbm,
           layer_hbm, fgrad_hbm, tgrad_hbm, wgrad_hbm,
           layer_s, fgrad_s, tgrad_s, wgrad_s,
           frames_s, cot_s, text_s, wq_s, wk_s, wv_s, wcat_s, wall_s,
           k_s, v_s, qt_s, ut_s, gk_s, gv_s, ends_s, att_s, dq_s,
           far_att, far_dq, edge_s, far_edge, kv_s, term_s, near_s, sum_c, far_x, sum_x, far_z,
           tterm_s, far_t, sum_f,
           load_w, load_f, load_c, store_sem,
           send_h, recv_h, send_wy, recv_wy, send_wz, recv_wz, send_wx, recv_wx, send_wc, recv_wc,
           send_a, recv_a, send_b, recv_b, send_e, recv_e, send_c, recv_c, send_x, recv_x, send_z, recv_z, send_t, recv_t):
    seq, head = lax.axis_index("seq"), lax.axis_index("head")
    core, x, z = seq % 2, (seq // 2) % 4, seq // 8
    y_of = lambda d: (head + d) % 4
    x_of = lambda d: (x + d) % 4
    z_of = lambda d: (z + d) % 8
    at_y = lambda d: (seq, y_of(d))
    at_x = lambda d: (z * 8 + x_of(d) * 2 + core, head)
    at_z = lambda d: (z_of(d) * 8 + x * 2 + core, head)
    at_core = (z * 8 + x * 2 + (1 - core), head)
    at_next = ((seq + 1) % RANGES, head)
    at_prev = ((seq + RANGES - 1) % RANGES, head)

    peers = [at_y(d) for d in (1, 2, 3)] + [at_x(d) for d in (1, 2, 3)] + [at_z(d) for d in range(1, 8)]
    peers += [at_core, at_next, at_prev]
    barrier = pltpu.get_barrier_semaphore()
    for peer in peers:
        pl.semaphore_signal(barrier, inc=1, device_id=peer, device_id_type=MESH)

    def load(src, dst, sem):
        copy = pltpu.make_async_copy(src, dst, sem)
        copy.start()
        return copy

    loads = [load(wq_hbm, wq_s, load_w.at[0]),
             load(wo_hbm, wcat_s.at[0], load_w.at[1]),
             load(text_hbm, text_s.at[pl.ds(WINDOW, S_DEV)], load_w.at[2]),
             load(wk_hbm, wk_s, load_w.at[3]),
             load(wv_hbm, wv_s, load_w.at[4])]

    def chunk(j, which):
        rows = pl.ds(pl.multiple_of(((head + jnp.where(j == 0, 2, jnp.where(j == 1, 1, jnp.where(j == 2, 3, 0)))) % 4) * TILE, TILE), TILE)
        if which == 0:
            return pltpu.make_async_copy(frames_hbm.at[rows], frames_s.at[rows], load_f.at[j])
        return pltpu.make_async_copy(cot_hbm.at[rows], cot_s.at[rows], load_c.at[j])

    for j in range(4):
        chunk(j, 0).start()
        chunk(j, 1).start()

    loads[0].wait()
    wcat_s[1] = jnp.transpose(wq_s[...])
    loads[1].wait()

    def remote(src, dst, sends, recvs, index, peer):
        return pltpu.make_async_remote_copy(src_ref=src, dst_ref=dst, send_sem=sends.at[index], recv_sem=recvs.at[index],
                                            device_id=peer, device_id_type=MESH)

    def send(*args):
        copy = remote(*args)
        copy.start()
        return copy

    pl.semaphore_wait(barrier, len(peers))
    halo = [send(text_hbm.at[pl.ds(S_DEV - WINDOW, WINDOW)], text_s.at[pl.ds(0, WINDOW)], send_h, recv_h, 0, at_next),
            send(text_hbm.at[pl.ds(0, WINDOW)], text_s.at[pl.ds(WINDOW + S_DEV, WINDOW)], send_h, recv_h, 1, at_prev)]
    by_x = pl.ds(pl.multiple_of(x * 32, 32), 32)
    by_z = pl.ds(pl.multiple_of(128 + z * 16, 16), 16)
    from_y = []
    for d in (1, 2, 3):
        from_y.append(send(wcat_s.at[core, by_x], wall_s.at[d - 1, core, by_x], send_wy, recv_wy, d - 1, at_y(d)))
        from_y.append(send(wcat_s.at[core, by_z], wall_s.at[d - 1, core, by_z], send_wy, recv_wy, d + 2, at_y(d)))

    def projections(j):
        chunk(j, 0).wait()
        chunk(j, 1).wait()
        rows = pl.ds(pl.multiple_of(((head + jnp.where(j == 0, 2, jnp.where(j == 1, 1, jnp.where(j == 2, 3, 0)))) % 4) * TILE, TILE), TILE)
        qt_s[:, rows] = mm(wcat_s[1], frames_s[rows, :], NT).astype(BF)
        ut_s[:, rows] = mm(wcat_s[0], cot_s[rows, :], NT).astype(BF)

    @pl.loop(0, 4)
    def _(j):
        projections(j)

    length = dur_ref[...]
    before = lax.broadcasted_iota(jnp.int32, (S_DEV, S_DEV), 1) <= lax.broadcasted_iota(jnp.int32, (S_DEV, S_DEV), 0)
    ends_s[...] = jnp.sum(jnp.where(before, jnp.broadcast_to(length, (S_DEV, S_DEV)), 0), axis=1, keepdims=True)
    gk_s[...] = jnp.zeros_like(gk_s)
    gv_s[...] = jnp.zeros_like(gv_s)
    for copy in loads[2:]:
        copy.wait()
    for copy in halo:
        copy.wait()
    keys = mm(text_s[...], wk_s[...], NN).astype(BF)
    vals = mm(text_s[...], wv_s[...], NN).astype(BF)
    for h in range(HEADS):
        k_s[h] = keys[:, h * HEAD_DIM:(h + 1) * HEAD_DIM]
        v_s[h] = vals[:, h * HEAD_DIM:(h + 1) * HEAD_DIM]
    first = jnp.where(seq == 0, WINDOW, 0)
    last = EXT - 1 - jnp.where(seq == RANGES - 1, WINDOW, 0)

    def place_of(i):
        if isinstance(i, int):
            return ((2, 0), (2, 1), (1, 0), (3, 0), (1, 1), (3, 1), (0, 0), (0, 1))[i]
        middle = (i >= 2) & (i < 6)
        d = jnp.where(middle, 1 + 2 * (i % 2), jnp.where(i < 2, 2, 0))
        return d, jnp.where(middle, (i - 2) // 2, i % 2)

    def exchange(i, which):
        d, part = place_of(i)
        peer_y = (head + d) % 4
        lanes = pl.ds(pl.multiple_of(peer_y * TILE + part * SUB, SUB), SUB)
        there = pl.ds(pl.multiple_of(part * SUB, SUB), SUB)
        if which == 0:
            return remote(att_s.at[:, lanes], far_att.at[d - 1, :, there], send_a, recv_a, i, (seq, peer_y))
        return remote(dq_s.at[:, lanes], far_dq.at[d - 1, :, there], send_b, recv_b, i, (seq, peer_y))

    slot_x, slot_z = wall_s.at[:, core, by_x], wall_s.at[:, core, by_z]
    from_x = [remote(slot_x, slot_x, send_wx, recv_wx, d - 1, at_x(d)) for d in (2, 1, 3)]
    from_z = [remote(slot_z, slot_z, send_wz, recv_wz, d - 1, at_z(d)) for d in (4, 3, 5, 2, 6, 1, 7)]

    @pl.loop(0, 8)
    def _(i):
        d, part = place_of(i)
        tile = ((head + d) % 4) * 2 + part
        @pl.when(i == 2)
        def _():
            for copy in from_y:
                copy.wait()
            for copy in from_z + from_x:
                copy.start()

        rows = pl.ds(pl.multiple_of(tile * SUB, SUB), SUB)
        start = pl.multiple_of((tile // 2) * 16, 16)
        here = pl.ds(start, SPAN)
        position = lax.broadcasted_iota(jnp.int32, (S_DEV, SUB), 1) + tile * SUB
        own = jnp.sum((ends_s[...] <= position).astype(jnp.int32), axis=0, keepdims=True)
        low = jnp.maximum(own, first)
        high = jnp.minimum(own + 2 * WINDOW, last)
        state = lax.broadcasted_iota(jnp.int32, (SPAN, SUB), 0) + start
        allowed = (state >= low) & (state <= high)
        hs = range(HEADS)
        cols = [pl.ds(h * HEAD_DIM, HEAD_DIM) for h in hs]
        q = [qt_s[cols[h], rows] for h in hs]
        u = [ut_s[cols[h], rows] for h in hs]
        k = [k_s[h, here, :] for h in hs]
        v = [v_s[h, here, :] for h in hs]
        s = [jnp.where(allowed, mm(k[h], q[h], NN), -jnp.inf) for h in hs]
        dp = [mm(v[h], u[h], NN) for h in hs]
        e = [jnp.exp2((s[h] - jnp.max(s[h], axis=0, keepdims=True)) * (LOG2E * HEAD_DIM ** -0.5)) for h in hs]
        p = [e[h] * (1.0 / jnp.sum(e[h], axis=0, keepdims=True)) for h in hs]
        pb = [p[h].astype(BF) for h in hs]
        att = [mm(v[h], pb[h], TN).astype(BF) for h in hs]
        for h in hs:
            att_s[cols[h], rows] = att[h]
        delta = [jnp.sum(u[h].astype(F32) * att[h].astype(F32), axis=0, keepdims=True) for h in hs]
        ds = [(p[h] * (dp[h] - delta[h]) * HEAD_DIM ** -0.5).astype(BF) for h in hs]
        for h in hs:
            gv_s[h, here, :] += mm(pb[h], u[h], NT)
        for h in hs:
            dq_s[cols[h], rows] = mm(k[h], ds[h], TN).astype(BF)
        for h in hs:
            gk_s[h, here, :] += mm(ds[h], q[h], NT)

        @pl.when(i < 6)
        def _():
            exchange(i, 0).start()

    for h in range(HEADS):
        cols = slice(h * HEAD_DIM, (h + 1) * HEAD_DIM)
        later = slice(COLS + h * HEAD_DIM, COLS + (h + 1) * HEAD_DIM)
        edge_s[0, :, cols] = gk_s[h, :WINDOW].astype(BF)
        edge_s[1, :, cols] = gk_s[h, WINDOW + S_DEV:].astype(BF)
        edge_s[0, :, later] = gv_s[h, :WINDOW].astype(BF)
        edge_s[1, :, later] = gv_s[h, WINDOW + S_DEV:].astype(BF)
    edge_copies = [send(edge_s.at[0], far_edge.at[0], send_e, recv_e, 0, at_prev),
                   send(edge_s.at[1], far_edge.at[1], send_e, recv_e, 1, at_next)]
    for i in range(6):
        exchange(i, 1).start()

    def put(group, value, block):
        for part in range(2):
            for chip in range(4):
                for side in range(2):
                    at = part * 128 + chip * 32 + side * 16
                    term_s[group, side, chip, block * 2 + part, :, :] = value[at:at + 16]

    def frame_term(group, left_s, right_s):
        @pl.loop(0, 4)
        def _(block):
            lanes = pl.ds(pl.multiple_of(block * 256, 256), 256)
            value = mm(left_s[...], right_s[:, lanes], NN)
            put(group, jnp.transpose(value).astype(BF), block)

    def core_send(group):
        return send(term_s.at[group, 1 - core], near_s.at[group], send_c, recv_c, group, at_core)

    x_copies, z_copies, core_copies = {}, {}, {}

    def chip_sum(group):
        core_copies[group].wait()

        @pl.loop(0, 4)
        def _(chip):
            sum_c[group, chip] = (term_s[group, core, chip].astype(F32) + near_s[group, chip].astype(F32)).astype(BF)
        x_copies[group] = [send(sum_c.at[group, x_of(d)], far_x.at[group, d - 1], send_x, recv_x, group * 3 + d - 1, at_x(d))
                           for d in (2, 1, 3)]

    def second_send(group):
        for copy in x_copies[group]:
            copy.wait()
        total = sum_c[group, x].astype(F32)
        for d in range(3):
            total = total + far_x[group, d].astype(F32)
        sum_x[group] = total.astype(BF)
        z_copies[group] = [send(sum_x.at[group, z_of(d)], far_z.at[group, d - 1], send_z, recv_z, group * 7 + d - 1, at_z(d))
                           for d in (4, 3, 5, 2, 6, 1, 7)]

    for h in range(HEADS):
        for at, grad in ((h * HEAD_DIM, gk_s), (COLS + h * HEAD_DIM, gv_s)):
            kv_s[:, at:at + HEAD_DIM] = grad[h].astype(BF)
    for which in range(2):
        @pl.loop(0, 4)
        def _(block):
            lanes = pl.ds(pl.multiple_of(block * 256, 256), 256)
            value = mm(text_s[:, lanes], kv_s[:, which * COLS:(which + 1) * COLS], TN)
            put(2 + which, value.astype(BF), block)
        core_copies[2 + which] = core_send(2 + which)
    frame_term(0, att_s, cot_s)
    core_copies[0] = core_send(0)
    chip_sum(2)
    chip_sum(3)
    frame_term(1, dq_s, frames_s)
    core_copies[1] = core_send(1)
    chip_sum(0)

    for copy in edge_copies:
        copy.wait()
    inner = slice(WINDOW, WINDOW + S_DEV)
    for h in range(HEADS):
        for at, grad in ((h * HEAD_DIM, gk_s), (COLS + h * HEAD_DIM, gv_s)):
            cols = slice(at, at + HEAD_DIM)
            grad[h, WINDOW:2 * WINDOW] += far_edge[1, :, cols].astype(F32)
            grad[h, S_DEV:WINDOW + S_DEV] += far_edge[0, :, cols].astype(F32)
            kv_s[inner, cols] = grad[h, inner].astype(BF)
    for part in range(4):
        rows = slice(WINDOW + part * 64, WINDOW + part * 64 + 64)
        value = mm(kv_s[rows, :COLS], wk_s[...], NT) + mm(kv_s[rows, COLS:], wv_s[...], NT)
        tterm_s[part] = value.astype(BF)
    text_copies = [send(tterm_s.at[y_of(d)], far_t.at[d - 1], send_t, recv_t, d - 1, at_y(d)) for d in (2, 1, 3)]
    chip_sum(1)

    for copy in from_x + from_z:
        copy.wait()
    from_core = send(wall_s.at[:, core], wall_s.at[:, core], send_wc, recv_wc, 0, at_core)
    second_send(2)
    second_send(3)
    second_send(0)

    def turned(mine_s, far, d):
        if d == 0:
            return jnp.transpose(mine_s[:, pl.ds(pl.multiple_of(head * TILE, TILE), TILE)])
        return jnp.transpose(far[d - 1])

    def term_of(part, which, d, lanes):
        weight = wcat_s[which, :, lanes] if d == 0 else wall_s[d - 1, which, :, lanes]
        return mm(part, weight, NN).astype(BF).astype(F32)

    blocks = [slice(n * 256, n * 256 + 256) for n in range(4)]

    from_core.wait()
    for i in range(6):
        exchange(i, 0).wait()
    parts = [turned(att_s, far_att, d) for d in range(4)]
    for lanes in blocks:
        total = term_of(parts[0], 0, 0, lanes)
        for d in (1, 2, 3):
            total = total + term_of(parts[d], 0, d, lanes)
        layer_s[:, lanes] = total.astype(BF)
    stores = [load(layer_s, layer_hbm, store_sem.at[0])]
    second_send(1)
    for i in (0, 1):
        exchange(i, 1).wait()
    parts = [turned(dq_s, far_dq, d) for d in (0, 2)]
    for lanes in blocks:
        sum_f[:, lanes] = term_of(parts[0], 1, 0, lanes) + term_of(parts[1], 1, 2, lanes)
    for i in (2, 4):
        exchange(i, 1).wait()
    part = turned(dq_s, far_dq, 1)
    for lanes in blocks:
        sum_f[:, lanes] = sum_f[:, lanes] + term_of(part, 1, 1, lanes)
    for i in (3, 5):
        exchange(i, 1).wait()
    part = turned(dq_s, far_dq, 3)
    for lanes in blocks:
        fgrad_s[:, lanes] = (sum_f[:, lanes] + term_of(part, 1, 3, lanes)).astype(BF)
    stores.append(load(fgrad_s, fgrad_hbm, store_sem.at[1]))

    for copy in text_copies:
        copy.wait()
    total = tterm_s[head].astype(F32)
    for d in range(3):
        total = total + far_t[d].astype(F32)
    tgrad_s[...] = total.astype(BF)
    stores.append(load(tgrad_s, tgrad_hbm, store_sem.at[2]))

    for group in (2, 3, 0, 1):
        for copy in z_copies[group]:
            copy.wait()
        total = sum_x[group, z].astype(F32)
        for d in range(7):
            total = total + far_z[group, d].astype(F32)
        wgrad_s[group] = total
    stores.append(load(wgrad_s, wgrad_hbm, store_sem.at[3]))
    for copy in stores:
        copy.wait()


def move_kernel(layer_in, fgrad_in, tgrad_in, wgrad_in, layer_out, fgrad_out, tgrad_out, w0, w1, w2, w3,
                layer_s, fgrad_s, tgrad_s, wgrad_s, into, out_of):
    pieces = []
    for part in range(4):
        rows = pl.ds(part * 128, 128)
        pieces.append((layer_in.at[rows], layer_s.at[rows], layer_out.at[rows]))
        pieces.append((fgrad_in.at[rows], fgrad_s.at[rows], fgrad_out.at[rows]))
    pieces.append((tgrad_in, tgrad_s, tgrad_out))
    for group, out in enumerate((w0, w1, w2, w3)):
        pieces.append((wgrad_in.at[group], wgrad_s.at[group], out))
    reads = [pltpu.make_async_copy(src, mid, into.at[n]) for n, (src, mid, _) in enumerate(pieces)]
    writes = [pltpu.make_async_copy(mid, dst, out_of.at[n]) for n, (_, mid, dst) in enumerate(pieces)]
    for copy in reads:
        copy.start()
    for read, write in zip(reads, writes):
        read.wait()
        write.start()
    for copy in writes:
        copy.wait()


def on_device(frames, text_states, durations, w_query, w_key, w_value, w_out, cotangent):
    vmem = pl.BlockSpec(memory_space=pltpu.VMEM)
    hbm = pl.BlockSpec(memory_space=pltpu.HBM)
    dma = pltpu.SemaphoreType.DMA
    layer, fgrad, tgrad, wgrad = pl.pallas_call(
        kernel,
        in_specs=[hbm] * 3 + [vmem] + [hbm] * 4,
        out_specs=[hbm] * 4,
        out_shape=[
            jax.ShapeDtypeStruct((TILE, D), BF),
            jax.ShapeDtypeStruct((TILE, D), BF),
            jax.ShapeDtypeStruct((64, D), BF),
            jax.ShapeDtypeStruct((4, 16, COLS), F32),
        ],
        scratch_shapes=[
            pltpu.VMEM((TILE, D), BF),
            pltpu.VMEM((TILE, D), BF),
            pltpu.VMEM((64, D), BF),
            pltpu.VMEM((4, 16, COLS), F32),
            pltpu.VMEM((F_DEV, D), BF),
            pltpu.VMEM((F_DEV, D), BF),
            pltpu.VMEM((EXT, D), BF),
            pltpu.VMEM((D, COLS), BF),
            pltpu.VMEM((D, COLS), BF),
            pltpu.VMEM((D, COLS), BF),
            pltpu.VMEM((2, COLS, D), BF),
            pltpu.VMEM((3, 2, COLS, D), BF),
            pltpu.VMEM((HEADS, EXT, HEAD_DIM), BF),
            pltpu.VMEM((HEADS, EXT, HEAD_DIM), BF),
            pltpu.VMEM((COLS, F_DEV), BF),
            pltpu.VMEM((COLS, F_DEV), BF),
            pltpu.VMEM((HEADS, EXT, HEAD_DIM), F32),
            pltpu.VMEM((HEADS, EXT, HEAD_DIM), F32),
            pltpu.VMEM((S_DEV, 1), jnp.int32),
            pltpu.VMEM((COLS, F_DEV), BF),
            pltpu.VMEM((COLS, F_DEV), BF),
            pltpu.VMEM((3, COLS, TILE), BF),
            pltpu.VMEM((3, COLS, TILE), BF),
            pltpu.VMEM((2, WINDOW, 2 * COLS), BF),
            pltpu.VMEM((2, WINDOW, 2 * COLS), BF),
            pltpu.VMEM((EXT, 2 * COLS), BF),
            pltpu.VMEM((4, 2, 4, 8, 16, COLS), BF),
            pltpu.VMEM((4, 4, 8, 16, COLS), BF),
            pltpu.VMEM((4, 4, 8, 16, COLS), BF),
            pltpu.VMEM((4, 3, 8, 16, COLS), BF),
            pltpu.VMEM((4, 8, 16, COLS), BF),
            pltpu.VMEM((4, 7, 16, COLS), BF),
            pltpu.VMEM((4, 64, D), BF),
            pltpu.VMEM((3, 64, D), BF),
            pltpu.VMEM((TILE, D), F32),
            dma((5,)), dma((4,)), dma((4,)), dma((4,)),
            dma((2,)), dma((2,)), dma((6,)), dma((6,)), dma((7,)), dma((7,)), dma((3,)), dma((3,)), dma((1,)), dma((1,)),
            dma((6,)), dma((6,)), dma((6,)), dma((6,)), dma((2,)), dma((2,)), dma((4,)), dma((4,)),
            dma((12,)), dma((12,)), dma((28,)), dma((28,)), dma((3,)), dma((3,)),
        ],
        compiler_params=pltpu.CompilerParams(collective_id=0, has_side_effects=True, vmem_limit_bytes=60 * 2 ** 20),
        cost_estimate=pl.CostEstimate(flops=15 * 10 ** 9, bytes_accessed=16 * 10 ** 6, transcendentals=3 * 10 ** 6),
    )(frames, cotangent, text_states, durations, w_query, w_key, w_value, w_out)
    small = jax.ShapeDtypeStruct((16, COLS), F32)
    layer, fgrad, tgrad, w0, w1, w2, w3 = pl.pallas_call(
        move_kernel,
        in_specs=[hbm] * 4,
        out_specs=[hbm] * 7,
        out_shape=[
            jax.ShapeDtypeStruct((TILE, D), BF),
            jax.ShapeDtypeStruct((TILE, D), BF),
            jax.ShapeDtypeStruct((64, D), BF),
            small, small, small, small,
        ],
        scratch_shapes=[
            pltpu.VMEM((TILE, D), BF),
            pltpu.VMEM((TILE, D), BF),
            pltpu.VMEM((64, D), BF),
            pltpu.VMEM((4, 16, COLS), F32),
            dma((13,)), dma((13,)),
        ],
        compiler_params=pltpu.CompilerParams(vmem_limit_bytes=60 * 2 ** 20),
        cost_estimate=pl.CostEstimate(flops=0, bytes_accessed=5 * 10 ** 6, transcendentals=0),
    )(layer, fgrad, tgrad, wgrad)
    return layer, fgrad, tgrad, w1, w2, w3, jnp.transpose(w0)


def solution(mesh):
    placed = (
        P("seq", None),
        P("seq", None),
        P("seq", None),
        P(None, "head"),
        P(None, "head"),
        P(None, "head"),
        P("head", None),
        P("seq", None),
    )
    return jax.shard_map(
        on_device,
        mesh=mesh,
        in_specs=placed,
        out_specs=(
            P(("seq", "head"), None),
            P(("seq", "head"), None),
            P(("seq", "head"), None),
            P("seq", "head"),
            P("seq", "head"),
            P("seq", "head"),
            P("head", "seq"),
        ),
        check_vma=False,
    )
```

```python
import jax
import jax.numpy as jnp
from jax import lax
from jax.experimental import pallas as pl
from jax.experimental.pallas import tpu as pltpu
from jax.sharding import PartitionSpec as P

HEAD_DIM = 64
WINDOW = 32
HEADS = 4
COLS = HEADS * HEAD_DIM
D = 1024
F_DEV = 2048
S_DEV = 256
EXT = S_DEV + 2 * WINDOW
TILE = 512
SUB = 256
SPAN = 272
RANGES = 64
LOG2E = 1.4426950408889634
MESH = pl.DeviceIdType.MESH
BF = jnp.bfloat16
F32 = jnp.float32
NN = (((1,), (0,)), ((), ()))
NT = (((1,), (1,)), ((), ()))
TN = (((0,), (0,)), ((), ()))


def mm(left, right, dims):
    return lax.dot_general(left, right, dims, preferred_element_type=F32)


def kernel(frames_hbm, cot_hbm, text_hbm, dur_ref, wq_hbm, wk_hbm, wv_hbm, wo_hbm,
           layer_hbm, fgrad_hbm, tgrad_hbm, wgrad_hbm,
           layer_s, fgrad_s, tgrad_s, wgrad_s,
           frames_s, cot_s, text_s, wq_s, wk_s, wv_s, wcat_s, wall_s,
           k_s, v_s, qt_s, ut_s, gk_s, gv_s, ends_s, att_s, dq_s,
           far_att, far_dq, edge_s, far_edge, kv_s, term_s, near_s, sum_c, far_x, sum_x, far_z, first_z, sum_z, last_x,
           tterm_s, far_t, sum_f,
           load_w, load_f, load_c, store_sem,
           send_h, recv_h, send_wy, recv_wy, send_wz, recv_wz, send_wx, recv_wx, send_wc, recv_wc,
           send_a, recv_a, send_b, recv_b, send_e, recv_e, send_c, recv_c, send_x, recv_x, send_z, recv_z, send_t, recv_t):
    seq, head = lax.axis_index("seq"), lax.axis_index("head")
    core, x, z = seq % 2, (seq // 2) % 4, seq // 8
    y_of = lambda d: (head + d) % 4
    x_of = lambda d: (x + d) % 4
    z_of = lambda d: (z + d) % 8
    at_y = lambda d: (seq, y_of(d))
    at_x = lambda d: (z * 8 + x_of(d) * 2 + core, head)
    at_z = lambda d: (z_of(d) * 8 + x * 2 + core, head)
    at_core = (z * 8 + x * 2 + (1 - core), head)
    at_next = ((seq + 1) % RANGES, head)
    at_prev = ((seq + RANGES - 1) % RANGES, head)

    peers = [at_y(d) for d in (1, 2, 3)] + [at_x(d) for d in (1, 2, 3)] + [at_z(d) for d in range(1, 8)]
    peers += [at_core, at_next, at_prev]
    barrier = pltpu.get_barrier_semaphore()
    for peer in peers:
        pl.semaphore_signal(barrier, inc=1, device_id=peer, device_id_type=MESH)

    def load(src, dst, sem):
        copy = pltpu.make_async_copy(src, dst, sem)
        copy.start()
        return copy

    loads = [load(wq_hbm, wq_s, load_w.at[0]),
             load(wo_hbm, wcat_s.at[0], load_w.at[1]),
             load(text_hbm, text_s.at[pl.ds(WINDOW, S_DEV)], load_w.at[2]),
             load(wk_hbm, wk_s, load_w.at[3]),
             load(wv_hbm, wv_s, load_w.at[4])]

    def chunk(j, which):
        rows = pl.ds(pl.multiple_of(((head + jnp.where(j == 0, 2, jnp.where(j == 1, 1, jnp.where(j == 2, 3, 0)))) % 4) * TILE, TILE), TILE)
        if which == 0:
            return pltpu.make_async_copy(frames_hbm.at[rows], frames_s.at[rows], load_f.at[j])
        return pltpu.make_async_copy(cot_hbm.at[rows], cot_s.at[rows], load_c.at[j])

    for j in range(4):
        chunk(j, 0).start()
        chunk(j, 1).start()

    loads[0].wait()
    wcat_s[1] = jnp.transpose(wq_s[...])
    loads[1].wait()

    def remote(src, dst, sends, recvs, index, peer):
        return pltpu.make_async_remote_copy(src_ref=src, dst_ref=dst, send_sem=sends.at[index], recv_sem=recvs.at[index],
                                            device_id=peer, device_id_type=MESH)

    def send(*args):
        copy = remote(*args)
        copy.start()
        return copy

    pl.semaphore_wait(barrier, len(peers))
    halo = [send(text_hbm.at[pl.ds(S_DEV - WINDOW, WINDOW)], text_s.at[pl.ds(0, WINDOW)], send_h, recv_h, 0, at_next),
            send(text_hbm.at[pl.ds(0, WINDOW)], text_s.at[pl.ds(WINDOW + S_DEV, WINDOW)], send_h, recv_h, 1, at_prev)]
    by_x = pl.ds(pl.multiple_of(x * 32, 32), 32)
    by_z = pl.ds(pl.multiple_of(128 + z * 16, 16), 16)
    from_y = []
    for d in (1, 2, 3):
        from_y.append(send(wcat_s.at[core, by_x], wall_s.at[d - 1, core, by_x], send_wy, recv_wy, d - 1, at_y(d)))
        from_y.append(send(wcat_s.at[core, by_z], wall_s.at[d - 1, core, by_z], send_wy, recv_wy, d + 2, at_y(d)))

    def projections(j):
        chunk(j, 0).wait()
        chunk(j, 1).wait()
        rows = pl.ds(pl.multiple_of(((head + jnp.where(j == 0, 2, jnp.where(j == 1, 1, jnp.where(j == 2, 3, 0)))) % 4) * TILE, TILE), TILE)
        qt_s[:, rows] = mm(wcat_s[1], frames_s[rows, :], NT).astype(BF)
        ut_s[:, rows] = mm(wcat_s[0], cot_s[rows, :], NT).astype(BF)

    @pl.loop(0, 4)
    def _(j):
        projections(j)

    length = dur_ref[...]
    before = lax.broadcasted_iota(jnp.int32, (S_DEV, S_DEV), 1) <= lax.broadcasted_iota(jnp.int32, (S_DEV, S_DEV), 0)
    ends_s[...] = jnp.sum(jnp.where(before, jnp.broadcast_to(length, (S_DEV, S_DEV)), 0), axis=1, keepdims=True)
    gk_s[...] = jnp.zeros_like(gk_s)
    gv_s[...] = jnp.zeros_like(gv_s)
    for copy in loads[2:]:
        copy.wait()
    for copy in halo:
        copy.wait()
    keys = mm(text_s[...], wk_s[...], NN).astype(BF)
    vals = mm(text_s[...], wv_s[...], NN).astype(BF)
    for h in range(HEADS):
        k_s[h] = keys[:, h * HEAD_DIM:(h + 1) * HEAD_DIM]
        v_s[h] = vals[:, h * HEAD_DIM:(h + 1) * HEAD_DIM]
    first = jnp.where(seq == 0, WINDOW, 0)
    last = EXT - 1 - jnp.where(seq == RANGES - 1, WINDOW, 0)

    def place_of(i):
        if isinstance(i, int):
            return ((2, 0), (2, 1), (1, 0), (3, 0), (1, 1), (3, 1), (0, 0), (0, 1))[i]
        middle = (i >= 2) & (i < 6)
        d = jnp.where(middle, 1 + 2 * (i % 2), jnp.where(i < 2, 2, 0))
        return d, jnp.where(middle, (i - 2) // 2, i % 2)

    def exchange(i, which):
        d, part = place_of(i)
        peer_y = (head + d) % 4
        lanes = pl.ds(pl.multiple_of(peer_y * TILE + part * SUB, SUB), SUB)
        there = pl.ds(pl.multiple_of(part * SUB, SUB), SUB)
        if which == 0:
            return remote(att_s.at[:, lanes], far_att.at[d - 1, :, there], send_a, recv_a, i, (seq, peer_y))
        return remote(dq_s.at[:, lanes], far_dq.at[d - 1, :, there], send_b, recv_b, i, (seq, peer_y))

    slot_x, slot_z = wall_s.at[:, core, by_x], wall_s.at[:, core, by_z]
    from_x = [remote(slot_x, slot_x, send_wx, recv_wx, d - 1, at_x(d)) for d in (2, 1, 3)]
    from_z = [remote(slot_z, slot_z, send_wz, recv_wz, d - 1, at_z(d)) for d in (4, 3, 5, 2, 6, 1, 7)]

    @pl.loop(0, 8)
    def _(i):
        d, part = place_of(i)
        tile = ((head + d) % 4) * 2 + part
        @pl.when(i == 2)
        def _():
            for copy in from_y:
                copy.wait()
            for copy in from_z + from_x:
                copy.start()

        rows = pl.ds(pl.multiple_of(tile * SUB, SUB), SUB)
        start = pl.multiple_of((tile // 2) * 16, 16)
        here = pl.ds(start, SPAN)
        position = lax.broadcasted_iota(jnp.int32, (S_DEV, SUB), 1) + tile * SUB
        own = jnp.sum((ends_s[...] <= position).astype(jnp.int32), axis=0, keepdims=True)
        low = jnp.maximum(own, first)
        high = jnp.minimum(own + 2 * WINDOW, last)
        state = lax.broadcasted_iota(jnp.int32, (SPAN, SUB), 0) + start
        allowed = (state >= low) & (state <= high)
        hs = range(HEADS)
        cols = [pl.ds(h * HEAD_DIM, HEAD_DIM) for h in hs]
        q = [qt_s[cols[h], rows] for h in hs]
        u = [ut_s[cols[h], rows] for h in hs]
        k = [k_s[h, here, :] for h in hs]
        v = [v_s[h, here, :] for h in hs]
        s = [jnp.where(allowed, mm(k[h], q[h], NN), -jnp.inf) for h in hs]
        dp = [mm(v[h], u[h], NN) for h in hs]
        e = [jnp.exp2((s[h] - jnp.max(s[h], axis=0, keepdims=True)) * (LOG2E * HEAD_DIM ** -0.5)) for h in hs]
        p = [e[h] * (1.0 / jnp.sum(e[h], axis=0, keepdims=True)) for h in hs]
        pb = [p[h].astype(BF) for h in hs]
        att = [mm(v[h], pb[h], TN).astype(BF) for h in hs]
        for h in hs:
            att_s[cols[h], rows] = att[h]
        delta = [jnp.sum(u[h].astype(F32) * att[h].astype(F32), axis=0, keepdims=True) for h in hs]
        ds = [(p[h] * (dp[h] - delta[h])).astype(BF) for h in hs]
        for h in hs:
            gv_s[h, here, :] += mm(pb[h], u[h], NT)
        for h in hs:
            dq_s[cols[h], rows] = (mm(k[h], ds[h], TN) * HEAD_DIM ** -0.5).astype(BF)
        for h in hs:
            gk_s[h, here, :] += mm(ds[h], q[h], NT)

        @pl.when(i < 6)
        def _():
            exchange(i, 0).start()

    gk_s[...] = gk_s[...] * HEAD_DIM ** -0.5
    for h in range(HEADS):
        cols = slice(h * HEAD_DIM, (h + 1) * HEAD_DIM)
        later = slice(COLS + h * HEAD_DIM, COLS + (h + 1) * HEAD_DIM)
        edge_s[0, :, cols] = gk_s[h, :WINDOW].astype(BF)
        edge_s[1, :, cols] = gk_s[h, WINDOW + S_DEV:].astype(BF)
        edge_s[0, :, later] = gv_s[h, :WINDOW].astype(BF)
        edge_s[1, :, later] = gv_s[h, WINDOW + S_DEV:].astype(BF)
    edge_copies = [send(edge_s.at[0], far_edge.at[0], send_e, recv_e, 0, at_prev),
                   send(edge_s.at[1], far_edge.at[1], send_e, recv_e, 1, at_next)]
    for i in range(6):
        exchange(i, 1).start()

    def put(group, value, block):
        parts = value.shape[0] // 128
        for part in range(parts):
            for chip in range(4):
                for side in range(2):
                    at = part * 128 + chip * 32 + side * 16
                    term_s[group, side, chip, block * parts + part, :, :] = value[at:at + 16]

    def frame_term(group, left_s, right_s):
        @pl.loop(0, 2)
        def _(block):
            lanes = pl.ds(pl.multiple_of(block * 512, 512), 512)
            value = mm(left_s[...], right_s[:, lanes], NN)
            put(group, jnp.transpose(value).astype(BF), block)

    def core_send(group):
        return send(term_s.at[group, 1 - core], near_s.at[group], send_c, recv_c, group, at_core)

    x_copies, z_copies, core_copies = {}, {}, {}

    def chip_sum(group):
        core_copies[group].wait()

        @pl.loop(0, 4)
        def _(chip):
            sum_c[group, chip] = (term_s[group, core, chip].astype(F32) + near_s[group, chip].astype(F32)).astype(BF)
        if group == 1:
            z_copies[group] = [send(sum_c.at[group, :, z_of(d)], first_z.at[d - 1], send_z, recv_z, group * 7 + d - 1, at_z(d))
                               for d in (4, 3, 5, 2, 6, 1, 7)]
            return
        x_copies[group] = [send(sum_c.at[group, x_of(d)], far_x.at[group, d - 1], send_x, recv_x, group * 3 + d - 1, at_x(d))
                           for d in (2, 1, 3)]

    def second_send(group):
        if group == 1:
            for copy in z_copies[group]:
                copy.wait()
            total = sum_c[group, :, z].astype(F32)
            for d in range(7):
                total = total + first_z[d].astype(F32)
            sum_z[...] = total.astype(BF)
            x_copies[group] = [send(sum_z.at[x_of(d)], last_x.at[d - 1], send_x, recv_x, group * 3 + d - 1, at_x(d)) for d in (2, 1, 3)]
            return
        for copy in x_copies[group]:
            copy.wait()
        total = sum_c[group, x].astype(F32)
        for d in range(3):
            total = total + far_x[group, d].astype(F32)
        sum_x[group] = total.astype(BF)
        z_copies[group] = [send(sum_x.at[group, z_of(d)], far_z.at[group, d - 1], send_z, recv_z, group * 7 + d - 1, at_z(d))
                           for d in (4, 3, 5, 2, 6, 1, 7)]

    for h in range(HEADS):
        for at, grad in ((h * HEAD_DIM, gk_s), (COLS + h * HEAD_DIM, gv_s)):
            kv_s[:, at:at + HEAD_DIM] = grad[h].astype(BF)
    @pl.loop(0, 4)
    def _(block):
        lanes = pl.ds(pl.multiple_of(block * 256, 256), 256)
        value = mm(text_s[:, lanes], kv_s[...], TN).astype(BF)
        put(2, value[:, :COLS], block)
        put(3, value[:, COLS:], block)
    core_copies[2] = core_send(2)
    core_copies[3] = core_send(3)
    frame_term(0, att_s, cot_s)
    core_copies[0] = core_send(0)
    chip_sum(2)
    chip_sum(3)
    frame_term(1, dq_s, frames_s)
    core_copies[1] = core_send(1)
    chip_sum(0)

    for copy in edge_copies:
        copy.wait()
    inner = slice(WINDOW, WINDOW + S_DEV)
    for h in range(HEADS):
        for at, grad in ((h * HEAD_DIM, gk_s), (COLS + h * HEAD_DIM, gv_s)):
            cols = slice(at, at + HEAD_DIM)
            grad[h, WINDOW:2 * WINDOW] += far_edge[1, :, cols].astype(F32)
            grad[h, S_DEV:WINDOW + S_DEV] += far_edge[0, :, cols].astype(F32)
            kv_s[inner, cols] = grad[h, inner].astype(BF)
    for part in range(4):
        rows = slice(WINDOW + part * 64, WINDOW + part * 64 + 64)
        value = mm(kv_s[rows, :COLS], wk_s[...], NT) + mm(kv_s[rows, COLS:], wv_s[...], NT)
        tterm_s[part] = value.astype(BF)
    text_copies = [send(tterm_s.at[y_of(d)], far_t.at[d - 1], send_t, recv_t, d - 1, at_y(d)) for d in (2, 1, 3)]
    chip_sum(1)

    for copy in from_x + from_z:
        copy.wait()
    from_core = send(wall_s.at[:, core], wall_s.at[:, core], send_wc, recv_wc, 0, at_core)
    second_send(2)
    second_send(3)
    second_send(0)

    def turned(mine_s, far, d):
        if d == 0:
            return jnp.transpose(mine_s[:, pl.ds(pl.multiple_of(head * TILE, TILE), TILE)])
        return jnp.transpose(far[d - 1])

    def term_of(part, which, d, lanes):
        weight = wcat_s[which, :, lanes] if d == 0 else wall_s[d - 1, which, :, lanes]
        return mm(part, weight, NN).astype(BF).astype(F32)

    blocks = [slice(n * 256, n * 256 + 256) for n in range(4)]

    from_core.wait()
    for i in range(6):
        exchange(i, 0).wait()
    parts = [turned(att_s, far_att, d) for d in range(4)]
    for lanes in blocks:
        total = term_of(parts[0], 0, 0, lanes)
        for d in (1, 2, 3):
            total = total + term_of(parts[d], 0, d, lanes)
        layer_s[:, lanes] = total.astype(BF)
    stores = [load(layer_s, layer_hbm, store_sem.at[0])]
    second_send(1)
    for i in (0, 1):
        exchange(i, 1).wait()
    parts = [turned(dq_s, far_dq, d) for d in (0, 2)]
    for lanes in blocks:
        sum_f[:, lanes] = term_of(parts[0], 1, 0, lanes) + term_of(parts[1], 1, 2, lanes)
    for i in (2, 4):
        exchange(i, 1).wait()
    part = turned(dq_s, far_dq, 1)
    for lanes in blocks:
        sum_f[:, lanes] = sum_f[:, lanes] + term_of(part, 1, 1, lanes)
    for i in (3, 5):
        exchange(i, 1).wait()
    part = turned(dq_s, far_dq, 3)
    for lanes in blocks:
        fgrad_s[:, lanes] = (sum_f[:, lanes] + term_of(part, 1, 3, lanes)).astype(BF)
    stores.append(load(fgrad_s, fgrad_hbm, store_sem.at[1]))

    for copy in text_copies:
        copy.wait()
    total = tterm_s[head].astype(F32)
    for d in range(3):
        total = total + far_t[d].astype(F32)
    tgrad_s[...] = total.astype(BF)
    stores.append(load(tgrad_s, tgrad_hbm, store_sem.at[2]))

    for group in (2, 3, 0):
        for copy in z_copies[group]:
            copy.wait()
        total = sum_x[group, z].astype(F32)
        for d in range(7):
            total = total + far_z[group, d].astype(F32)
        wgrad_s[group] = total
    for copy in x_copies[1]:
        copy.wait()
    total = sum_z[x].astype(F32)
    for d in range(3):
        total = total + last_x[d].astype(F32)
    wgrad_s[1] = total
    stores.append(load(wgrad_s, wgrad_hbm, store_sem.at[3]))
    for copy in stores:
        copy.wait()


def move_kernel(layer_in, fgrad_in, tgrad_in, wgrad_in, layer_out, fgrad_out, tgrad_out, w0, w1, w2, w3,
                layer_s, fgrad_s, tgrad_s, wgrad_s, into, out_of):
    pieces = []
    for part in range(4):
        rows = pl.ds(part * 128, 128)
        pieces.append((layer_in.at[rows], layer_s.at[rows], layer_out.at[rows]))
        pieces.append((fgrad_in.at[rows], fgrad_s.at[rows], fgrad_out.at[rows]))
    pieces.append((tgrad_in, tgrad_s, tgrad_out))
    for group, out in enumerate((w0, w1, w2, w3)):
        pieces.append((wgrad_in.at[group], wgrad_s.at[group], out))
    reads = [pltpu.make_async_copy(src, mid, into.at[n]) for n, (src, mid, _) in enumerate(pieces)]
    writes = [pltpu.make_async_copy(mid, dst, out_of.at[n]) for n, (_, mid, dst) in enumerate(pieces)]
    for copy in reads:
        copy.start()
    for read, write in zip(reads, writes):
        read.wait()
        write.start()
    for copy in writes:
        copy.wait()


def on_device(frames, text_states, durations, w_query, w_key, w_value, w_out, cotangent):
    vmem = pl.BlockSpec(memory_space=pltpu.VMEM)
    hbm = pl.BlockSpec(memory_space=pltpu.HBM)
    dma = pltpu.SemaphoreType.DMA
    layer, fgrad, tgrad, wgrad = pl.pallas_call(
        kernel,
        in_specs=[hbm] * 3 + [vmem] + [hbm] * 4,
        out_specs=[hbm] * 4,
        out_shape=[
            jax.ShapeDtypeStruct((TILE, D), BF),
            jax.ShapeDtypeStruct((TILE, D), BF),
            jax.ShapeDtypeStruct((64, D), BF),
            jax.ShapeDtypeStruct((4, 16, COLS), F32),
        ],
        scratch_shapes=[
            pltpu.VMEM((TILE, D), BF),
            pltpu.VMEM((TILE, D), BF),
            pltpu.VMEM((64, D), BF),
            pltpu.VMEM((4, 16, COLS), F32),
            pltpu.VMEM((F_DEV, D), BF),
            pltpu.VMEM((F_DEV, D), BF),
            pltpu.VMEM((EXT, D), BF),
            pltpu.VMEM((D, COLS), BF),
            pltpu.VMEM((D, COLS), BF),
            pltpu.VMEM((D, COLS), BF),
            pltpu.VMEM((2, COLS, D), BF),
            pltpu.VMEM((3, 2, COLS, D), BF),
            pltpu.VMEM((HEADS, EXT, HEAD_DIM), BF),
            pltpu.VMEM((HEADS, EXT, HEAD_DIM), BF),
            pltpu.VMEM((COLS, F_DEV), BF),
            pltpu.VMEM((COLS, F_DEV), BF),
            pltpu.VMEM((HEADS, EXT, HEAD_DIM), F32),
            pltpu.VMEM((HEADS, EXT, HEAD_DIM), F32),
            pltpu.VMEM((S_DEV, 1), jnp.int32),
            pltpu.VMEM((COLS, F_DEV), BF),
            pltpu.VMEM((COLS, F_DEV), BF),
            pltpu.VMEM((3, COLS, TILE), BF),
            pltpu.VMEM((3, COLS, TILE), BF),
            pltpu.VMEM((2, WINDOW, 2 * COLS), BF),
            pltpu.VMEM((2, WINDOW, 2 * COLS), BF),
            pltpu.VMEM((EXT, 2 * COLS), BF),
            pltpu.VMEM((4, 2, 4, 8, 16, COLS), BF),
            pltpu.VMEM((4, 4, 8, 16, COLS), BF),
            pltpu.VMEM((4, 4, 8, 16, COLS), BF),
            pltpu.VMEM((4, 3, 8, 16, COLS), BF),
            pltpu.VMEM((4, 8, 16, COLS), BF),
            pltpu.VMEM((4, 7, 16, COLS), BF),
            pltpu.VMEM((7, 4, 16, COLS), BF),
            pltpu.VMEM((4, 16, COLS), BF),
            pltpu.VMEM((3, 16, COLS), BF),
            pltpu.VMEM((4, 64, D), BF),
            pltpu.VMEM((3, 64, D), BF),
            pltpu.VMEM((TILE, D), F32),
            dma((5,)), dma((4,)), dma((4,)), dma((4,)),
            dma((2,)), dma((2,)), dma((6,)), dma((6,)), dma((7,)), dma((7,)), dma((3,)), dma((3,)), dma((1,)), dma((1,)),
            dma((6,)), dma((6,)), dma((6,)), dma((6,)), dma((2,)), dma((2,)), dma((4,)), dma((4,)),
            dma((12,)), dma((12,)), dma((28,)), dma((28,)), dma((3,)), dma((3,)),
        ],
        compiler_params=pltpu.CompilerParams(collective_id=0, has_side_effects=True, vmem_limit_bytes=60 * 2 ** 20),
        cost_estimate=pl.CostEstimate(flops=15 * 10 ** 9, bytes_accessed=16 * 10 ** 6, transcendentals=3 * 10 ** 6),
    )(frames, cotangent, text_states, durations, w_query, w_key, w_value, w_out)
    small = jax.ShapeDtypeStruct((16, COLS), F32)
    layer, fgrad, tgrad, w0, w1, w2, w3 = pl.pallas_call(
        move_kernel,
        in_specs=[hbm] * 4,
        out_specs=[hbm] * 7,
        out_shape=[
            jax.ShapeDtypeStruct((TILE, D), BF),
            jax.ShapeDtypeStruct((TILE, D), BF),
            jax.ShapeDtypeStruct((64, D), BF),
            small, small, small, small,
        ],
        scratch_shapes=[
            pltpu.VMEM((TILE, D), BF),
            pltpu.VMEM((TILE, D), BF),
            pltpu.VMEM((64, D), BF),
            pltpu.VMEM((4, 16, COLS), F32),
            dma((13,)), dma((13,)),
        ],
        compiler_params=pltpu.CompilerParams(vmem_limit_bytes=60 * 2 ** 20),
        cost_estimate=pl.CostEstimate(flops=0, bytes_accessed=5 * 10 ** 6, transcendentals=0),
    )(layer, fgrad, tgrad, wgrad)
    return layer, fgrad, tgrad, w1, w2, w3, jnp.transpose(w0)


def solution(mesh):
    placed = (
        P("seq", None),
        P("seq", None),
        P("seq", None),
        P(None, "head"),
        P(None, "head"),
        P(None, "head"),
        P("head", None),
        P("seq", None),
    )
    return jax.shard_map(
        on_device,
        mesh=mesh,
        in_specs=placed,
        out_specs=(
            P(("seq", "head"), None),
            P(("seq", "head"), None),
            P(("seq", "head"), None),
            P("seq", "head"),
            P("seq", "head"),
            P("seq", "head"),
            P("head", "seq"),
        ),
        check_vma=False,
    )
```
